128 devices in a mesh: section: 16 (over y_hi, x, core), tp: 8 (over z, y_lo).
Axes of the slice: x: 4, y: 4 (y_hi: 2, y_lo: 2; y = y_hi * 2 + y_lo), z: 4, core: 2. Of those that a mesh axis runs over, the one named last changes fastest.
Arguments:
- inputs: bfloat16 [16, 1024, 3584], P('section', 'tp'), may hold values from -6 to 6
- norm_gain: float32 [16, 3584], P('section'), may hold values from 0.5 to 1.5
- incoming_grad: bfloat16 [16, 1024, 3584], P('section', 'tp'), may hold values from -6 to 6
- up_tiles: bfloat16 [16, 784, 128, 128], P('section', 'tp'), may hold values from -0.1875 to 0.1875
- up_index: int32 [16, 784, 2], P('section', 'tp'), may hold values from 0 to 27, as said below
- up_count: int32 [16, 8], P('section', 'tp'), may hold values from 49 to 98, as said below
- down_tiles: bfloat16 [16, 784, 128, 128], P('section', 'tp'), may hold values from -0.09375 to 0.09375
- down_index: int32 [16, 784, 2], P('section', 'tp'), may hold values from 0 to 27, as said below
- down_count: int32 [16, 8], P('section', 'tp'), may hold values from 49 to 98, as said below
Outputs:
- input_grad: bfloat16 [16, 1024, 3584], P('section', 'tp')
- up_grad: bfloat16 [16, 784, 128, 128], P('section', 'tp')
- down_grad: bfloat16 [16, 784, 128, 128], P('section', 'tp')
The draws below stay inside these ranges and needn't reach their ends.
Inputs may be any that keep to these rules, and one draw needn't show every extreme that they name: `up_index`: each shard's list names 98 different blocks: column 0 a feature block below 28, column 1 a unit block below 14. `down_index`: each shard's list names 98 different blocks: column 0 a unit block below 14, column 1 a feature block below 28. Only the first up_count entries of a shard's list are kept blocks. In every section some shard has all 98. Only the first down_count entries of a shard's list are kept blocks. In every section some shard has all 98.
All inputs are finite; a program needn't handle non-finite values.
Results may differ from the reference program's by a relative error of at most 0.012.
Values may be sent and summed in bfloat16 or wider, within the bound.
No kernel may reach another device: no remote copies, remote signals or barrier semaphores. Data moves between devices by JAX's collectives and lax.ppermute only.
A program may use at most 256 MiB of HBM per device.

```python
import jax
import jax.numpy as jnp
from jax import lax

D = 3584
FF = 14336
BLK = 128
SECTIONS = 16
GROUP = 8
TOKENS = 1024
RB = 28
CB = 14
TILES = 98


def index_lists(key, first_blocks, second_blocks):
    keys = jax.random.split(key, SECTIONS * GROUP)

    def one_list(list_key):
        return jax.random.permutation(list_key, jnp.arange(first_blocks * second_blocks, dtype=jnp.int32))[:TILES]
    picks = jax.vmap(one_list)(keys)
    pairs = jnp.stack([picks // second_blocks, picks % second_blocks], axis=-1)
    return pairs.reshape(SECTIONS, GROUP * TILES, 2).astype(jnp.int32)


def stack_counts(key):
    first_key, second_key = jax.random.split(key)
    counts = jax.random.randint(first_key, (SECTIONS, GROUP), TILES // 2, TILES + 1)
    full_shard = jax.random.randint(second_key, (SECTIONS, 1), 0, GROUP)
    shard_ids = jnp.arange(GROUP, dtype=jnp.int32)[None, :]
    return jnp.where(shard_ids == full_shard, TILES, counts).astype(jnp.int32)


def draw_up_index(key, part):
    key = jax.random.fold_in(key, 11)
    return index_lists(key, RB, CB)


def draw_down_index(key, part):
    key = jax.random.fold_in(key, 23)
    return index_lists(key, CB, RB)


def draw_up_count(key, part):
    key = jax.random.fold_in(key, 37)
    return stack_counts(key)


def draw_down_count(key, part):
    key = jax.random.fold_in(key, 41)
    return stack_counts(key)


def block_levels(rng, shape, shards, least, top_value):
    level, own = 1.0, jax.random.fold_in(rng, 6)
    for position, parts in shards:
        steps = jnp.exp(jax.random.uniform(jax.random.fold_in(own, position), (parts,), jnp.float32, least / len(shards), top_value / len(shards)))
        level = level * jnp.repeat(steps, shape[position] // parts).reshape([-1 if axis == position else 1 for axis in range(len(shape))])
    return level


def scatter_about(rng, shape, deviation, limit, cuts=(), held_as=jnp.bfloat16):
    loudness = block_levels(rng, shape, cuts, -0.22, 0.18) if cuts else 1.0
    result = jax.random.normal(rng, shape, jnp.float32) * deviation * loudness
    return jnp.minimum(jnp.maximum(result, -limit), limit).astype(held_as)


def setup_inputs(seed: int = 0) -> dict:
    key_of = jax.random.split(jax.random.key(seed), 10)
    return {
        "inputs": scatter_about(key_of[0], (SECTIONS, TOKENS, D), 1.0, 6.0, ((0, 16), (1, 8))),
        "norm_gain": jnp.clip(1.0 + 0.1 * jax.random.normal(key_of[1], (SECTIONS, D), jnp.float32), 0.5, 1.5),
        "incoming_grad": scatter_about(key_of[2], (SECTIONS, TOKENS, D), 1.0, 6.0, ((0, 16), (1, 8))),
        "up_tiles": scatter_about(key_of[3], (SECTIONS, GROUP * TILES, BLK, BLK), (D // 4) ** -0.5, 0.1875, ((0, 16), (1, 8))),
        "up_index": draw_up_index(jax.random.fold_in(key_of[9], 71), 0),
        "up_count": draw_up_count(jax.random.fold_in(key_of[9], 71), 0),
        "down_tiles": scatter_about(key_of[6], (SECTIONS, GROUP * TILES, BLK, BLK), (FF // 4) ** -0.5, 0.09375, ((0, 16), (1, 8))),
        "down_index": draw_down_index(jax.random.fold_in(key_of[9], 71), 0),
        "down_count": draw_down_count(jax.random.fold_in(key_of[9], 71), 0),
    }


EPS = 1e-05
GELU_C = 0.7978845608028654

def gelu_value(pre_act):
    inner = jnp.tanh(GELU_C * (pre_act + 0.044715 * pre_act * pre_act * pre_act))
    return 0.5 * pre_act * (1.0 + inner)

def gelu_slope(pre_act):
    inner = jnp.tanh(GELU_C * (pre_act + 0.044715 * pre_act * pre_act * pre_act))
    return 0.5 * (1.0 + inner) + 0.5 * pre_act * (1.0 - inner * inner) * GELU_C * (1.0 + 3.0 * 0.044715 * pre_act * pre_act)

def place_blocks(product, put_index, kept_mask, block_count):
    placing = ((put_index[:, None] == jnp.arange(block_count, dtype=jnp.int32)[None, :]) & kept_mask[:, None]).astype(jnp.float32)
    spread = jnp.einsum('tkc,kj->tjc', product, placing, precision=lax.Precision.HIGHEST)
    return spread.reshape(product.shape[0], block_count * product.shape[2])

def tile_product(left, tiles, take_index, put_index, kept_mask, block_count, form):
    row_count = left.shape[0]
    tile_side = tiles.shape[-1]
    picked = jnp.take(left.reshape(row_count, -1, tile_side), take_index, axis=1).astype(jnp.float32)
    product = jnp.einsum(form, picked, tiles.astype(jnp.float32), precision=lax.Precision.HIGHEST)
    return place_blocks(product, put_index, kept_mask, block_count)

def tile_outer(left, right, left_index, right_index, kept_mask):
    row_count = left.shape[0]
    tile_side = BLK
    left_pick = jnp.take(left.reshape(row_count, -1, tile_side), left_index, axis=1).astype(jnp.float32)
    right_pick = jnp.take(right.reshape(row_count, -1, tile_side), right_index, axis=1).astype(jnp.float32)
    summed = jnp.einsum('tkb,tkc->kbc', left_pick, right_pick, precision=lax.Precision.HIGHEST)
    return jnp.where(kept_mask[:, None, None], summed, 0.0).astype(jnp.bfloat16)

def one_section(operands):
    section_in, gain, grad, up_tiles, up_index, up_count, down_tiles, down_index, down_count = operands
    inputs_f = section_in.astype(jnp.float32)
    rms_inv = lax.rsqrt(lax.optimization_barrier(jnp.mean(inputs_f * inputs_f, axis=-1, keepdims=True)) + EPS)
    normed = inputs_f * rms_inv
    units = (normed * gain[None, :]).astype(jnp.bfloat16)
    feature_blocks = D // BLK
    unit_blocks = FF // GROUP // BLK
    unit_grad = jnp.zeros((TOKENS, D), jnp.float32)
    up_parts = []
    down_parts = []
    for shard in range(GROUP):
        first = shard * TILES
        up_t = up_tiles[first:first + TILES]
        up_i = up_index[first:first + TILES]
        up_kept = jnp.arange(TILES, dtype=jnp.int32) < up_count[shard]
        down_t = down_tiles[first:first + TILES]
        down_i = down_index[first:first + TILES]
        down_kept = jnp.arange(TILES, dtype=jnp.int32) < down_count[shard]
        pre = tile_product(units, up_t, up_i[:, 0], up_i[:, 1], up_kept, unit_blocks, 'tkb,kbc->tkc')
        hidden = gelu_value(pre).astype(jnp.bfloat16)
        hidden_grad = tile_product(grad, down_t, down_i[:, 1], down_i[:, 0], down_kept, unit_blocks, 'tkb,kcb->tkc')
        pre_grad = (hidden_grad * gelu_slope(pre)).astype(jnp.bfloat16)
        up_parts.append(tile_outer(units, pre_grad, up_i[:, 0], up_i[:, 1], up_kept))
        down_parts.append(tile_outer(hidden, grad, down_i[:, 0], down_i[:, 1], down_kept))
        shard_term = tile_product(pre_grad, up_t, up_i[:, 1], up_i[:, 0], up_kept, feature_blocks, 'tkb,kcb->tkc')
        unit_grad = unit_grad + lax.optimization_barrier(shard_term.astype(jnp.bfloat16)).astype(jnp.float32)
    scaled = unit_grad * gain[None, :]
    normal_part = rms_inv * (scaled - normed * lax.optimization_barrier(jnp.mean(scaled * normed, axis=-1, keepdims=True)))
    input_grad = (grad.astype(jnp.float32) + normal_part).astype(jnp.bfloat16)
    return (input_grad, jnp.concatenate(up_parts, axis=0), jnp.concatenate(down_parts, axis=0))

def reference(inputs, norm_gain, incoming_grad, up_tiles, up_index, up_count, down_tiles, down_index, down_count):
    grads = jnp.roll(incoming_grad, -1, axis=0)
    input_grad, up_grad, down_grad = lax.map(one_section, (inputs, norm_gain, grads, up_tiles, up_index, up_count, down_tiles, down_index, down_count))
    return (input_grad, up_grad, down_grad)
```

```python
import functools

import jax
import jax.numpy as jnp
from jax import lax
from jax.experimental import pallas as pl
from jax.experimental.pallas import tpu as pltpu
from jax.sharding import PartitionSpec as P

FF = 14336
EPS = 1e-05
GELU_C = 0.7978845608028654
F32 = jnp.float32
BF16 = jnp.bfloat16
SIDE = 128
PAIR = 2
OFFSETS = (0, 1, -1, 2)
ANY = pl.BlockSpec(memory_space=pl.ANY)
VMEM = pl.BlockSpec(memory_space=pltpu.VMEM)
SMEM = pl.BlockSpec(memory_space=pltpu.SMEM)
ROOM = 60 * 1024 * 1024


def along_z(value, steps):
    count = lax.axis_size("tp")
    return lax.ppermute(value, "tp", [(i, (i + 2 * steps) % count) for i in range(count)])


def along_y(value):
    return lax.ppermute(value, "tp", [(i, i ^ 1) for i in range(lax.axis_size("tp"))])


def from_next_section(value):
    count = lax.axis_size("section")
    return lax.ppermute(value, "section", [(i, (i - 1) % count) for i in range(count)])


def plus(left, right):
    return (left.astype(F32) + right.astype(F32)).astype(BF16)


def lanes(block):
    return pl.ds(pl.multiple_of(block * SIDE, SIDE), SIDE)


def rounded_up(value, step):
    return -(-value // step) * step


def group_lists(index, count, key_column, width):
    length = index.shape[0]
    key, other = index[:, key_column], index[:, 1 - key_column]
    entry = jnp.arange(length, dtype=jnp.int32)
    live = entry < count
    same = (key[:, None] == key[None, :]) & live[None, :] & (entry[None, :] < entry[:, None])
    rank = jnp.sum(same.astype(jnp.int32), axis=1)
    opens = live & (rank % PAIR == 0)
    before = jnp.sum(((key[None, :] < key[:, None]) & opens[None, :]).astype(jnp.int32), axis=1)
    place = jnp.where(live, before * PAIR + rank, -1)
    at = jnp.arange(width, dtype=jnp.int32)
    empty = length * 32
    code = entry * 32 + other - empty
    codes = empty + jnp.sum(jnp.where(place[:, None] == at[None, :], code[:, None], 0), axis=0)
    keys = jnp.sum(jnp.where(place[:, None] == at[None, :] * PAIR, key[:, None], 0), axis=0)
    return codes, keys


def normed_kernel(inputs_ref, gain_ref, *unit_refs):
    rows = unit_refs[0].shape[0]
    for half, out_ref in enumerate(unit_refs):

        @pl.loop(0, rows // 16)
        def _(i):
            start = pl.multiple_of(i * 16, 16)
            value = inputs_ref[pl.ds(half * rows + start, 16), :].astype(F32)
            rms_inv = lax.rsqrt(jnp.mean(value * value, axis=-1, keepdims=True) + EPS)
            out_ref[pl.ds(start, 16), :] = (value * rms_inv * gain_ref[...]).astype(BF16)


def normed_units(inputs, gain, halves):
    rows, features = inputs.shape
    shape = jax.ShapeDtypeStruct((rows // halves, features), BF16)
    return pl.pallas_call(
        normed_kernel,
        out_shape=[shape] * halves,
        in_specs=[VMEM, VMEM],
        out_specs=[VMEM] * halves,
        compiler_params=pltpu.CompilerParams(vmem_limit_bytes=ROOM),
        cost_estimate=pl.CostEstimate(flops=0, bytes_accessed=4 * rows * features, transcendentals=0),
    )(inputs, gain)


def run_groups(count, unroll, one):
    whole = count // unroll

    @pl.loop(0, whole)
    def _(i):
        for j in range(unroll):
            one(i * unroll + j)

    for s in range(whole * unroll, count):
        one(s)


def start_tiles(tiles_ref, held, sem):
    count = tiles_ref.shape[0]
    copy = pltpu.make_async_copy(tiles_ref, held.at[pl.ds(0, count)], sem)
    copy.start()
    held[count] = jnp.zeros(held.shape[1:], BF16)
    return copy


def hidden_kernel(
    pieces, groups, codes_ref, keys_ref, *refs
):
    (unit_refs, grad_refs) = refs[: 2 * pieces], refs[2 * pieces : 3 * pieces]
    up_ref, down_ref, hidden_ref, pre_grad_ref = refs[3 * pieces : 3 * pieces + 4]
    units, grads, up, down, pre, hidden_grad, sems = refs[3 * pieces + 4 :]
    rows = unit_refs[0].shape[0]
    width = codes_ref.shape[1]
    copies = [start_tiles(up_ref, up, sems.at[0])]
    for i, ref in enumerate(unit_refs):
        copies.append(pltpu.make_async_copy(ref, units.at[pl.ds(i * rows, rows)], sems.at[1 + i]))
        copies[-1].start()
    late = [start_tiles(down_ref, down, sems.at[1 + 2 * pieces])]
    for i, ref in enumerate(grad_refs):
        for j in range(2):
            late.append(
                pltpu.make_async_copy(
                    ref.at[pl.ds(j * rows, rows)],
                    grads.at[pl.ds((j * pieces + i) * rows, rows)],
                    sems.at[2 + 2 * pieces + 2 * i + j],
                )
            )
            late[-1].start()
    pre[...] = jnp.zeros_like(pre)
    hidden_grad[...] = jnp.zeros_like(hidden_grad)
    for copy in copies:
        copy.wait()

    def add_pre(s):
        codes = [codes_ref[0, s * PAIR + i] for i in range(PAIR)]
        left = jnp.concatenate([units[:, lanes(code & 31)] for code in codes], axis=1)
        right = jnp.concatenate([up[code >> 5] for code in codes], axis=0)
        pre[:, lanes(keys_ref[0, s])] += jnp.dot(left, right, preferred_element_type=F32)

    run_groups(groups, 8, add_pre)
    for copy in late:
        copy.wait()

    def add_hidden_grad(s):
        codes = [codes_ref[1, s * PAIR + i] for i in range(PAIR)]
        left = jnp.concatenate([grads[:, lanes(code & 31)] for code in codes], axis=1)
        right = jnp.concatenate([down[code >> 5] for code in codes], axis=1)
        hidden_grad[:, lanes(keys_ref[1, s])] += lax.dot_general(
            left, right, (((1,), (1,)), ((), ())), preferred_element_type=F32
        )

    run_groups(groups, 8, add_hidden_grad)

    @pl.loop(0, pre.shape[0] // 32)
    def _(i):
        at = pl.ds(pl.multiple_of(i * 32, 32), 32)
        z = pre[at, :]
        square = z * z
        inner = jnp.tanh(GELU_C * (z + 0.044715 * square * z))
        hidden_ref[at, :] = (0.5 * z * (1.0 + inner)).astype(BF16)
        slope = 0.5 * (1.0 + inner) + 0.5 * z * (1.0 - inner * inner) * GELU_C * (
            1.0 + 3.0 * 0.044715 * square
        )
        pre_grad_ref[at, :] = (hidden_grad[at, :] * slope).astype(BF16)


def hidden_of(codes, keys, units, grads, up_tiles, down_tiles, unit_blocks, groups):
    pieces = len(grads)
    rows, features = units[0].shape
    tokens, wide = 2 * pieces * rows, unit_blocks * SIDE
    held = (up_tiles.shape[0] + 1,) + up_tiles.shape[1:]
    shape = jax.ShapeDtypeStruct((tokens, wide), BF16)
    flops = 4 * groups * PAIR * tokens * SIDE * SIDE
    return pl.pallas_call(
        functools.partial(hidden_kernel, pieces, groups),
        out_shape=[shape, shape],
        in_specs=[SMEM, SMEM] + [ANY] * (3 * pieces + 2),
        out_specs=[VMEM, VMEM],
        scratch_shapes=[
            pltpu.VMEM((tokens, features), BF16),
            pltpu.VMEM((tokens, features), BF16),
            pltpu.VMEM(held, BF16),
            pltpu.VMEM(held, BF16),
            pltpu.VMEM((tokens, wide), F32),
            pltpu.VMEM((tokens, wide), F32),
            pltpu.SemaphoreType.DMA((2 + 4 * pieces,)),
        ],
        compiler_params=pltpu.CompilerParams(vmem_limit_bytes=ROOM),
        cost_estimate=pl.CostEstimate(
            flops=4 * flops, bytes_accessed=4 * tokens * features, transcendentals=tokens * wide
        ),
    )(codes, keys, *units, *grads, up_tiles, down_tiles)


def unit_grad_kernel(groups, spans, codes_ref, keys_ref, pre_grad_ref, up_ref, *refs):
    out_refs = refs[: len(spans)]
    up, total, sem = refs[len(spans) :]
    copy = start_tiles(up_ref, up, sem.at[0])
    total[...] = jnp.zeros_like(total)
    copy.wait()

    def add(s):
        codes = [codes_ref[2, s * PAIR + i] for i in range(PAIR)]
        left = jnp.concatenate([pre_grad_ref[:, lanes(code & 31)] for code in codes], axis=1)
        right = jnp.concatenate([up[code >> 5] for code in codes], axis=1)
        total[:, lanes(keys_ref[2, s])] += lax.dot_general(
            left, right, (((1,), (1,)), ((), ())), preferred_element_type=F32
        )

    run_groups(groups, 9, add)
    for out_ref, parts in zip(out_refs, spans, strict=True):
        done = 0
        for start, size in parts:

            @pl.loop(0, size // 16)
            def _(i):
                step = pl.multiple_of(i * 16, 16)
                out_ref[pl.ds(done + step, 16), :] = total[pl.ds(start + step, 16), :].astype(BF16)

            done += size


def unit_grad_of(codes, keys, pre_grad, up_tiles, features, groups, spans):
    tokens = pre_grad.shape[0]
    held = (up_tiles.shape[0] + 1,) + up_tiles.shape[1:]
    flops = 2 * groups * PAIR * tokens * SIDE * SIDE
    return pl.pallas_call(
        functools.partial(unit_grad_kernel, groups, spans),
        out_shape=[
            jax.ShapeDtypeStruct((sum(size for _, size in parts), features), BF16) for parts in spans
        ],
        in_specs=[SMEM, SMEM, VMEM, ANY],
        out_specs=[VMEM] * len(spans),
        scratch_shapes=[
            pltpu.VMEM(held, BF16),
            pltpu.VMEM((tokens, features), F32),
            pltpu.SemaphoreType.DMA((1,)),
        ],
        compiler_params=pltpu.CompilerParams(vmem_limit_bytes=ROOM),
        cost_estimate=pl.CostEstimate(
            flops=4 * flops, bytes_accessed=2 * tokens * features, transcendentals=0
        ),
    )(codes, keys, pre_grad, up_tiles)


def up_grad_kernel(pieces, groups, codes_ref, keys_ref, *refs):
    unit_refs, slope_refs = refs[:pieces], refs[pieces : pieces + 2]
    out_ref, units, slopes, held, sems = refs[pieces + 2 :]
    rows, half = unit_refs[0].shape[0], slope_refs[0].shape[0]
    copies = []
    for i, ref in enumerate(unit_refs):
        copies.append(pltpu.make_async_copy(ref, units.at[pl.ds(i * rows, rows)], sems.at[i]))
    for i, ref in enumerate(slope_refs):
        copies.append(
            pltpu.make_async_copy(ref, slopes.at[pl.ds(i * half, half)], sems.at[pieces + i])
        )
    for copy in copies:
        copy.start()
    held[...] = jnp.zeros_like(held)
    for copy in copies:
        copy.wait()

    def one(s):
        codes = [codes_ref[0, s * PAIR + i] for i in range(PAIR)]
        left = jnp.concatenate([units[:, lanes(code & 31)] for code in codes], axis=1)
        summed = lax.dot_general(
            left,
            slopes[:, lanes(keys_ref[0, s])],
            (((0,), (0,)), ((), ())),
            preferred_element_type=F32,
        ).astype(BF16)
        for i, code in enumerate(codes):
            held[code >> 5] = summed[i * SIDE : (i + 1) * SIDE]

    run_groups(groups, 8, one)
    copy = pltpu.make_async_copy(held.at[pl.ds(0, out_ref.shape[0])], out_ref, sems.at[0])
    copy.start()
    copy.wait()


def up_grad_of(codes, keys, units, slopes, count, groups):
    pieces = len(units)
    rows, features = units[0].shape
    tokens, wide = pieces * rows, slopes[0].shape[1]
    flops = 2 * groups * PAIR * tokens * SIDE * SIDE
    return pl.pallas_call(
        functools.partial(up_grad_kernel, pieces, groups),
        out_shape=jax.ShapeDtypeStruct((count, SIDE, SIDE), BF16),
        in_specs=[SMEM, SMEM] + [ANY] * (pieces + 2),
        out_specs=ANY,
        scratch_shapes=[
            pltpu.VMEM((tokens, features), BF16),
            pltpu.VMEM((tokens, wide), BF16),
            pltpu.VMEM((count + 1, SIDE, SIDE), BF16),
            pltpu.SemaphoreType.DMA((pieces + 2,)),
        ],
        compiler_params=pltpu.CompilerParams(vmem_limit_bytes=ROOM),
        cost_estimate=pl.CostEstimate(
            flops=4 * flops, bytes_accessed=2 * tokens * features, transcendentals=0
        ),
    )(codes, keys, *units, *slopes)


def down_grad_kernel(pieces, groups, codes_ref, keys_ref, *refs):
    grad_refs, hidden_refs = refs[:pieces], refs[pieces : pieces + 2]
    out_ref, grads, hidden, turned, held, sems = refs[pieces + 2 :]
    rows, half = grad_refs[0].shape[0] // 2, hidden_refs[0].shape[0]
    each = pieces // 2
    copies = []
    for i, ref in enumerate(hidden_refs):
        copies.append(pltpu.make_async_copy(ref, hidden.at[pl.ds(i * half, half)], sems.at[i]))
    late = []
    for i, ref in enumerate(grad_refs):
        for j in range(2):
            at = (i // each) * half + (j * each + i % each) * rows
            late.append(
                pltpu.make_async_copy(
                    ref.at[pl.ds(j * rows, rows)],
                    grads.at[pl.ds(at, rows)],
                    sems.at[2 + 2 * i + j],
                )
            )
    for copy in copies + late:
        copy.start()
    held[...] = jnp.zeros_like(held)
    for copy in copies:
        copy.wait()

    @pl.loop(0, turned.shape[0])
    def _(c):
        turned[c] = hidden[:, lanes(c)].T

    for copy in late:
        copy.wait()

    def one(s):
        codes = [codes_ref[1, s * PAIR + i] for i in range(PAIR)]
        right = jnp.concatenate([grads[:, lanes(code & 31)] for code in codes], axis=1)
        summed = jnp.dot(turned[keys_ref[1, s]], right, preferred_element_type=F32).astype(BF16)
        for i, code in enumerate(codes):
            held[code >> 5] = summed[:, i * SIDE : (i + 1) * SIDE]

    run_groups(groups, 8, one)
    copy = pltpu.make_async_copy(held.at[pl.ds(0, out_ref.shape[0])], out_ref, sems.at[0])
    copy.start()
    copy.wait()


def down_grad_of(codes, keys, grads, hidden, count, groups):
    pieces = len(grads)
    rows, features = grads[0].shape
    tokens, wide = pieces * rows, hidden[0].shape[1]
    flops = 2 * groups * PAIR * tokens * SIDE * SIDE
    return pl.pallas_call(
        functools.partial(down_grad_kernel, pieces, groups),
        out_shape=jax.ShapeDtypeStruct((count, SIDE, SIDE), BF16),
        in_specs=[SMEM, SMEM] + [ANY] * (pieces + 2),
        out_specs=ANY,
        scratch_shapes=[
            pltpu.VMEM((tokens, features), BF16),
            pltpu.VMEM((tokens, wide), BF16),
            pltpu.VMEM((wide // SIDE, SIDE, tokens), BF16),
            pltpu.VMEM((count + 1, SIDE, SIDE), BF16),
            pltpu.SemaphoreType.DMA((2 + 2 * pieces,)),
        ],
        compiler_params=pltpu.CompilerParams(vmem_limit_bytes=ROOM),
        cost_estimate=pl.CostEstimate(
            flops=4 * flops, bytes_accessed=2 * tokens * features, transcendentals=0
        ),
    )(codes, keys, *grads, *hidden)


def input_grad_kernel(terms, inputs_ref, gain_ref, *refs):
    halves = len(terms)
    grad_refs, out_ref = refs[:halves], refs[-1]
    used = halves
    rows = grad_refs[0].shape[0]
    for half, count in enumerate(terms):
        term_refs = refs[used : used + count]
        used += count

        @pl.loop(0, rows // 16)
        def _(i):
            start = pl.multiple_of(i * 16, 16)
            here = pl.ds(start, 16)
            value = inputs_ref[pl.ds(half * rows + start, 16), :].astype(F32)
            rms_inv = lax.rsqrt(jnp.mean(value * value, axis=-1, keepdims=True) + EPS)
            normed = value * rms_inv
            unit_grad = term_refs[0][here, :].astype(F32)
            for ref in term_refs[1:]:
                unit_grad = unit_grad + ref[here, :].astype(F32)
            scaled = unit_grad * gain_ref[...]
            mean = jnp.mean(scaled * normed, axis=-1, keepdims=True)
            result = grad_refs[half][here, :].astype(F32) + rms_inv * (scaled - normed * mean)
            out_ref[pl.ds(half * rows + start, 16), :] = result.astype(BF16)


def input_grad_of(inputs, gain, arriving, terms):
    rows, features = inputs.shape
    flat = [term for half in terms for term in half]
    return pl.pallas_call(
        functools.partial(input_grad_kernel, tuple(len(half) for half in terms)),
        out_shape=jax.ShapeDtypeStruct((rows, features), BF16),
        in_specs=[VMEM] * (2 + len(arriving) + len(flat)),
        out_specs=VMEM,
        compiler_params=pltpu.CompilerParams(vmem_limit_bytes=ROOM),
        cost_estimate=pl.CostEstimate(flops=0, bytes_accessed=8 * rows * features, transcendentals=0),
    )(inputs, gain, *arriving, *flat)


def gathered_units(own, way):
    ahead, behind = along_z(own, -1), along_z(own, 1)
    far = along_z(behind, 1) if way > 0 else along_z(ahead, -1)
    same = [own, ahead, behind, far]
    return same + [along_y(piece) for piece in same]


def gathered_grads(own, way):
    both = jnp.concatenate([own, along_y(own)], axis=0)
    ahead, behind = along_z(both, -1), along_z(both, 1)
    far = along_z(behind, 1) if way > 0 else along_z(ahead, -1)
    return [both, ahead, behind, far]


def summed_along_z(parts, way):
    here, ahead, behind, far = parts
    if way > 0:
        one = along_z(plus(ahead, along_z(far, 1)), 1)
        two = along_z(behind, -1)
    else:
        one = along_z(plus(behind, along_z(far, -1)), -1)
        two = along_z(ahead, 1)
    return [here, one, two]


def body(
    inputs,
    norm_gain,
    incoming_grad,
    up_tiles,
    up_index,
    up_count,
    down_tiles,
    down_index,
    down_count,
):
    up, down = up_tiles[0], down_tiles[0]
    rows, features = inputs.shape[1:]
    count = up.shape[0]
    feature_blocks = features // SIDE
    unit_blocks = FF // lax.axis_size("tp") // SIDE
    by_unit = (count + unit_blocks * (PAIR - 1)) // PAIR
    by_feature = (count + feature_blocks * (PAIR - 1)) // PAIR
    width = rounded_up(PAIR * by_feature, SIDE)
    half = rows // 2
    halves = range(2)

    arriving = [from_next_section(incoming_grad[0, h * half : (h + 1) * half]) for h in halves]
    own_units = normed_units(inputs[0], norm_gain, 2)
    lists = [
        group_lists(up_index[0], up_count[0, 0], 1, width),
        group_lists(down_index[0], down_count[0, 0], 0, width),
        group_lists(up_index[0], up_count[0, 0], 0, width),
    ]
    codes = jnp.stack([pair[0] for pair in lists])
    keys = jnp.stack([pair[1] for pair in lists])

    units = [gathered_units(own_units[h], 1 - 2 * h) for h in halves]
    grads = [gathered_grads(arriving[h], 2 * h - 1) for h in halves]
    hidden, pre_grad, terms = [], [], []
    pieces = len(OFFSETS)
    for h in halves:
        one, two = hidden_of(codes, keys, units[h], grads[h], up, down, unit_blocks, by_unit)
        hidden.append(one)
        pre_grad.append(two)
        if h == 0:
            spans = [((pieces * half, pieces * half),)]
            spans += [((i * half, half),) for i in range(pieces)]
            sent, *kept = unit_grad_of(codes, keys, two, up, features, by_feature, tuple(spans))
            came = along_y(sent)
            parts = [plus(kept[i], came[i * half : (i + 1) * half]) for i in range(pieces)]
            terms.append(summed_along_z(parts, 1))
        else:
            spans = [((i * half, half), ((pieces + i) * half, half)) for i in range(pieces)]
            parts = unit_grad_of(codes, keys, two, up, features, by_feature, tuple(spans))
            sums = summed_along_z(parts, -1)
            other = (
                sums[0][half:].astype(F32) + sums[1][half:].astype(F32) + sums[2][half:].astype(F32)
            )
            terms.append([value[:half] for value in sums] + [along_y(other.astype(BF16))])
    up_grad = up_grad_of(codes, keys, units[0] + units[1], pre_grad, count, by_unit)
    down_grad = down_grad_of(codes, keys, grads[0] + grads[1], hidden, count, by_unit)
    input_grad = input_grad_of(inputs[0], norm_gain, arriving, terms)
    return (input_grad[None], up_grad[None], down_grad[None])


def solution(mesh):
    placed = (
        P("section", "tp", None),
        P("section", None),
        P("section", "tp", None),
        P("section", "tp", None, None),
        P("section", "tp", None),
        P("section", "tp"),
        P("section", "tp", None, None),
        P("section", "tp", None),
        P("section", "tp"),
    )
    return jax.shard_map(
        body,
        mesh=mesh,
        in_specs=placed,
        out_specs=(
            P("section", "tp", None),
            P("section", "tp", None, None),
            P("section", "tp", None, None),
        ),
        check_vma=False,
    )
```

```python
import functools

import jax
import jax.numpy as jnp
from jax import lax
from jax.experimental import pallas as pl
from jax.experimental.pallas import tpu as pltpu
from jax.sharding import PartitionSpec as P

FF = 14336
EPS = 1e-05
GELU_C = 0.7978845608028654
F32 = jnp.float32
BF16 = jnp.bfloat16
SIDE = 128
PAIR = 2
TREE = (
    (0, "y", "-"),
    (0, "+", "+"),
    (0, "-", "y"),
    (2, "+", "y"),
    (1, "-", "-"),
    (1, "+", "y"),
    (5, "-", "y"),
)
PIECES = 4
BACK = {"y": "y", "+": "-", "-": "+"}
ANY = pl.BlockSpec(memory_space=pl.ANY)
VMEM = pl.BlockSpec(memory_space=pltpu.VMEM)
SMEM = pl.BlockSpec(memory_space=pltpu.SMEM)
ROOM = 60 * 1024 * 1024
SMALL = pl.CostEstimate(flops=1024, bytes_accessed=1024, transcendentals=0)


def along(value, paths):
    sections, count = lax.axis_size("section"), lax.axis_size("tp")
    pairs = []
    for section in range(sections):
        for i in range(count):
            target = i
            for link in paths[section % 2]:
                target = target ^ 1 if link == "y" else (target + (2 if link == "+" else -2)) % count
            pairs.append((section * count + i, section * count + target))
    return lax.ppermute(value, ("section", "tp"), pairs)


def after(value, *earlier):
    return lax.optimization_barrier((value, *earlier))[0]


def from_next_section(value):
    count = lax.axis_size("section")
    return lax.ppermute(value, "section", [(i, (i - 1) % count) for i in range(count)])


def spread(pieces, steps, *earlier):
    for i in steps:
        parent, *links = TREE[i - 1]
        value = after(pieces[parent], *earlier) if earlier else pieces[parent]
        pieces[i] = along(value, links)


def returned(value, piece, until=0):
    paths = ["", ""]
    while piece != until:
        piece, *links = TREE[piece - 1]
        paths = [path + BACK[link] for path, link in zip(paths, links, strict=True)]
    return along(value, paths)


def lanes(block):
    return pl.ds(pl.multiple_of(block * SIDE, SIDE), SIDE)


def rounded_up(value, step):
    return -(-value // step) * step


def group_lists(index, count, key_column, width):
    length = index.shape[0]
    key, other = index[:, key_column], index[:, 1 - key_column]
    entry = jnp.arange(length, dtype=jnp.int32)
    live = entry < count
    same = (key[:, None] == key[None, :]) & live[None, :] & (entry[None, :] < entry[:, None])
    rank = jnp.sum(same.astype(jnp.int32), axis=1)
    opens = live & (rank % PAIR == 0)
    before = jnp.sum(((key[None, :] < key[:, None]) & opens[None, :]).astype(jnp.int32), axis=1)
    place = jnp.where(live, before * PAIR + rank, -1)
    at = jnp.arange(width, dtype=jnp.int32)
    empty = length * 32
    code = entry * 32 + other - empty
    codes = empty + jnp.sum(jnp.where(place[:, None] == at[None, :], code[:, None], 0), axis=0)
    keys = jnp.sum(jnp.where(place[:, None] == at[None, :] * PAIR, key[:, None], 0), axis=0)
    return codes, keys


def normed_kernel(inputs_ref, gain_ref, units_ref):
    for start in range(0, units_ref.shape[0], 16):
        at = pl.ds(start, 16)
        value = inputs_ref[at, :].astype(F32)
        rms_inv = lax.rsqrt(jnp.mean(value * value, axis=-1, keepdims=True) + EPS)
        units_ref[at, :] = (value * rms_inv * gain_ref[...]).astype(BF16)


def row_blocks(rows, features):
    return pl.BlockSpec((rows, features), lambda i: (i, 0))


def normed_units(inputs, gain):
    rows, features = inputs.shape
    return pl.pallas_call(
        normed_kernel,
        out_shape=jax.ShapeDtypeStruct((rows, features), BF16),
        grid=(rows // 32,),
        in_specs=[row_blocks(32, features), pl.BlockSpec((1, features), lambda i: (0, 0))],
        out_specs=row_blocks(32, features),
        compiler_params=pltpu.CompilerParams(vmem_limit_bytes=ROOM),
        cost_estimate=SMALL,
    )(inputs, gain)


def run_groups(count, unroll, one):
    whole = count // unroll

    @pl.loop(0, whole)
    def _(i):
        for j in range(unroll):
            one(i * unroll + j)

    for s in range(whole * unroll, count):
        one(s)


def start_tiles(tiles_ref, held, sem):
    count = tiles_ref.shape[0]
    copy = pltpu.make_async_copy(tiles_ref, held.at[pl.ds(0, count)], sem)
    copy.start()
    held[count] = jnp.zeros(held.shape[1:], BF16)
    return copy


def hidden_kernel(groups, codes_ref, keys_ref, *refs):
    unit_refs, (up_ref, hidden_ref, slope_ref, units, up, pre, sems) = refs[:PIECES], refs[PIECES:]
    rows = units.shape[0] // PIECES
    copies = [start_tiles(up_ref, up, sems.at[PIECES])]
    for i, ref in enumerate(unit_refs):
        copies.append(
            pltpu.make_async_copy(
                ref, units.at[pl.ds(i * rows, rows)], sems.at[i]
            )
        )
        copies[-1].start()
    pre[...] = jnp.zeros_like(pre)
    for copy in copies:
        copy.wait()

    def add(s):
        codes = [codes_ref[0, s * PAIR + i] for i in range(PAIR)]
        left = jnp.concatenate([units[:, lanes(code & 31)] for code in codes], axis=1)
        right = jnp.concatenate([up[code >> 5] for code in codes], axis=0)
        pre[:, lanes(keys_ref[0, s])] += jnp.dot(left, right, preferred_element_type=F32)

    run_groups(groups, 14, add)

    @pl.loop(0, pre.shape[0] // 32)
    def _(i):
        at = pl.ds(pl.multiple_of(i * 32, 32), 32)
        z = pre[at, :]
        square = z * z
        inner = jnp.tanh(GELU_C * (z + 0.044715 * square * z))
        hidden_ref[at, :] = (0.5 * z * (1.0 + inner)).astype(BF16)
        slope_ref[at, :] = 0.5 * (1.0 + inner) + 0.5 * z * (1.0 - inner * inner) * GELU_C * (
            1.0 + 3.0 * 0.044715 * square
        )


def hidden_of(codes, keys, units, up_tiles, unit_blocks, groups):
    rows, features = units[0].shape
    tokens, wide = PIECES * rows, unit_blocks * SIDE
    held = (up_tiles.shape[0] + 1,) + up_tiles.shape[1:]
    return pl.pallas_call(
        functools.partial(hidden_kernel, groups),
        out_shape=[
            jax.ShapeDtypeStruct((tokens, wide), BF16),
            jax.ShapeDtypeStruct((tokens, wide), F32),
        ],
        in_specs=[SMEM, SMEM] + [ANY] * (PIECES + 1),
        out_specs=[VMEM, VMEM],
        scratch_shapes=[
            pltpu.VMEM((tokens, features), BF16),
            pltpu.VMEM(held, BF16),
            pltpu.VMEM((tokens, wide), F32),
            pltpu.SemaphoreType.DMA((PIECES + 1,)),
        ],
        compiler_params=pltpu.CompilerParams(vmem_limit_bytes=ROOM),
        cost_estimate=SMALL,
    )(codes, keys, *units, up_tiles)


def pre_grad_kernel(pieces, start, groups, codes_ref, keys_ref, *refs):
    grad_refs, (down_ref, slope_ref, pre_grad_ref) = refs[:pieces], refs[pieces : pieces + 3]
    grads, down, slope, hidden_grad, sems = refs[pieces + 3 :]
    rows = grad_refs[0].shape[0]
    copies = [start_tiles(down_ref, down, sems.at[pieces])]
    for i, ref in enumerate(grad_refs):
        copies.append(
            pltpu.make_async_copy(ref, grads.at[pl.ds(i * rows, rows)], sems.at[i])
        )
        copies[-1].start()
    late = pltpu.make_async_copy(
        slope_ref.at[pl.ds(start, slope.shape[0])], slope, sems.at[pieces + 1]
    )
    late.start()
    hidden_grad[...] = jnp.zeros_like(hidden_grad)
    for copy in copies:
        copy.wait()

    def add(s):
        codes = [codes_ref[1, s * PAIR + i] for i in range(PAIR)]
        left = jnp.concatenate([grads[:, lanes(code & 31)] for code in codes], axis=1)
        right = jnp.concatenate([down[code >> 5] for code in codes], axis=1)
        hidden_grad[:, lanes(keys_ref[1, s])] += lax.dot_general(
            left, right, (((1,), (1,)), ((), ())), preferred_element_type=F32
        )

    run_groups(groups, 14, add)
    late.wait()

    @pl.loop(0, slope.shape[0] // 32)
    def _(i):
        at = pl.ds(pl.multiple_of(i * 32, 32), 32)
        pre_grad_ref[at, :] = (hidden_grad[at, :] * slope[at, :]).astype(BF16)


def pre_grad_of(codes, keys, grads, down_tiles, slope, groups, start=0):
    pieces = len(grads)
    rows, features = grads[0].shape
    tokens, wide = pieces * rows, slope.shape[1]
    held = (down_tiles.shape[0] + 1,) + down_tiles.shape[1:]
    return pl.pallas_call(
        functools.partial(pre_grad_kernel, pieces, start, groups),
        out_shape=jax.ShapeDtypeStruct((tokens, wide), BF16),
        in_specs=[SMEM, SMEM] + [ANY] * (pieces + 2),
        out_specs=VMEM,
        scratch_shapes=[
            pltpu.VMEM((tokens, features), BF16),
            pltpu.VMEM(held, BF16),
            pltpu.VMEM((tokens, wide), F32),
            pltpu.VMEM((tokens, wide), F32),
            pltpu.SemaphoreType.DMA((pieces + 2,)),
        ],
        compiler_params=pltpu.CompilerParams(vmem_limit_bytes=ROOM),
        cost_estimate=SMALL,
    )(codes, keys, *grads, down_tiles, slope)


def unit_grad_kernel(pieces, groups, codes_ref, keys_ref, pre_grad_ref, up_ref, *refs):
    out_refs, (up, total, sem) = refs[:pieces], refs[pieces:]
    rows = out_refs[0].shape[0]
    copy = start_tiles(up_ref, up, sem.at[0])
    total[...] = jnp.zeros_like(total)
    copy.wait()

    def add(s):
        codes = [codes_ref[2, s * PAIR + i] for i in range(PAIR)]
        left = jnp.concatenate([pre_grad_ref[:, lanes(code & 31)] for code in codes], axis=1)
        right = jnp.concatenate([up[code >> 5] for code in codes], axis=1)
        total[:, lanes(keys_ref[2, s])] += lax.dot_general(
            left, right, (((1,), (1,)), ((), ())), preferred_element_type=F32
        )

    run_groups(groups, 21, add)
    for piece, out_ref in enumerate(out_refs):

        @pl.loop(0, rows // 16)
        def _(i):
            step = pl.multiple_of(i * 16, 16)
            out_ref[pl.ds(step, 16), :] = total[pl.ds(piece * rows + step, 16), :].astype(BF16)


def unit_grad_of(codes, keys, pre_grad, up_tiles, rows, features, groups):
    tokens = pre_grad.shape[0]
    pieces = tokens // rows
    held = (up_tiles.shape[0] + 1,) + up_tiles.shape[1:]
    return pl.pallas_call(
        functools.partial(unit_grad_kernel, pieces, groups),
        out_shape=[jax.ShapeDtypeStruct((rows, features), BF16)] * pieces,
        in_specs=[SMEM, SMEM, VMEM, ANY],
        out_specs=[VMEM] * pieces,
        scratch_shapes=[
            pltpu.VMEM(held, BF16),
            pltpu.VMEM((tokens, features), F32),
            pltpu.SemaphoreType.DMA((1,)),
        ],
        compiler_params=pltpu.CompilerParams(vmem_limit_bytes=ROOM),
        cost_estimate=SMALL,
    )(codes, keys, pre_grad, up_tiles)


def up_grad_kernel(parts, groups, codes_ref, keys_ref, *refs):
    pieces = 2 * PIECES
    unit_refs, slope_refs = refs[:pieces], refs[pieces : pieces + parts]
    out_ref, units, slopes, held, sems = refs[pieces + parts :]
    rows, done = unit_refs[0].shape[0], 0
    copies = []
    for i, ref in enumerate(slope_refs):
        size = ref.shape[0]
        copies.append(
            pltpu.make_async_copy(ref, slopes.at[pl.ds(done, size)], sems.at[pieces + i])
        )
        done += size
    for i, ref in enumerate(unit_refs):
        copies.append(
            pltpu.make_async_copy(ref, units.at[pl.ds(i * rows, rows)], sems.at[i])
        )
    for copy in copies:
        copy.start()
    held[...] = jnp.zeros_like(held)
    for copy in copies:
        copy.wait()

    def one(s):
        codes = [codes_ref[0, s * PAIR + i] for i in range(PAIR)]
        left = jnp.concatenate([units[:, lanes(code & 31)] for code in codes], axis=1)
        summed = lax.dot_general(
            left,
            slopes[:, lanes(keys_ref[0, s])],
            (((0,), (0,)), ((), ())),
            preferred_element_type=F32,
        ).astype(BF16)
        for i, code in enumerate(codes):
            held[code >> 5] = summed[i * SIDE : (i + 1) * SIDE]

    run_groups(groups, 14, one)
    copy = pltpu.make_async_copy(held.at[pl.ds(0, out_ref.shape[0])], out_ref, sems.at[0])
    copy.start()
    copy.wait()


def up_grad_of(codes, keys, units, slopes, count, groups):
    pieces = len(units)
    rows, features = units[0].shape
    tokens, wide = pieces * rows, slopes[0].shape[1]
    return pl.pallas_call(
        functools.partial(up_grad_kernel, len(slopes), groups),
        out_shape=jax.ShapeDtypeStruct((count, SIDE, SIDE), BF16),
        in_specs=[SMEM, SMEM] + [ANY] * (pieces + len(slopes)),
        out_specs=ANY,
        scratch_shapes=[
            pltpu.VMEM((tokens, features), BF16),
            pltpu.VMEM((tokens, wide), BF16),
            pltpu.VMEM((count + 1, SIDE, SIDE), BF16),
            pltpu.SemaphoreType.DMA((pieces + len(slopes),)),
        ],
        compiler_params=pltpu.CompilerParams(vmem_limit_bytes=ROOM),
        cost_estimate=SMALL,
    )(codes, keys, *units, *slopes)


def down_grad_kernel(groups, codes_ref, keys_ref, *refs):
    pieces = 2 * PIECES
    grad_refs, hidden_refs = refs[:pieces], refs[pieces : pieces + 2]
    out_ref, grads, hidden, turned, held, sems = refs[pieces + 2 :]
    rows, half = grad_refs[0].shape[0], hidden_refs[0].shape[0]
    copies = []
    for i, ref in enumerate(hidden_refs):
        copies.append(pltpu.make_async_copy(ref, hidden.at[pl.ds(i * half, half)], sems.at[i]))
    late = []
    for i, ref in enumerate(grad_refs):
        late.append(
            pltpu.make_async_copy(ref, grads.at[pl.ds(i * rows, rows)], sems.at[2 + i])
        )
    for copy in copies + late:
        copy.start()
    held[...] = jnp.zeros_like(held)
    for copy in copies:
        copy.wait()

    @pl.loop(0, turned.shape[0])
    def _(c):
        turned[c] = hidden[:, lanes(c)].T

    for copy in late:
        copy.wait()

    def one(s):
        codes = [codes_ref[1, s * PAIR + i] for i in range(PAIR)]
        right = jnp.concatenate([grads[:, lanes(code & 31)] for code in codes], axis=1)
        summed = jnp.dot(turned[keys_ref[1, s]], right, preferred_element_type=F32).astype(BF16)
        for i, code in enumerate(codes):
            held[code >> 5] = summed[:, i * SIDE : (i + 1) * SIDE]

    run_groups(groups, 14, one)
    copy = pltpu.make_async_copy(held.at[pl.ds(0, out_ref.shape[0])], out_ref, sems.at[0])
    copy.start()
    copy.wait()


def down_grad_of(codes, keys, grads, hidden, count, groups):
    pieces = len(grads)
    rows, features = grads[0].shape
    tokens, wide = pieces * rows, hidden[0].shape[1]
    return pl.pallas_call(
        functools.partial(down_grad_kernel, groups),
        out_shape=jax.ShapeDtypeStruct((count, SIDE, SIDE), BF16),
        in_specs=[SMEM, SMEM] + [ANY] * (pieces + 2),
        out_specs=ANY,
        scratch_shapes=[
            pltpu.VMEM((tokens, features), BF16),
            pltpu.VMEM((tokens, wide), BF16),
            pltpu.VMEM((wide // SIDE, SIDE, tokens), BF16),
            pltpu.VMEM((count + 1, SIDE, SIDE), BF16),
            pltpu.SemaphoreType.DMA((2 + pieces,)),
        ],
        compiler_params=pltpu.CompilerParams(vmem_limit_bytes=ROOM),
        cost_estimate=SMALL,
    )(codes, keys, *grads, *hidden)


def input_grad_kernel(inputs_ref, gain_ref, grad_ref, *refs):
    term_refs, out_ref = refs[:-1], refs[-1]
    for start in range(0, out_ref.shape[0], 16):
        here = pl.ds(start, 16)
        value = inputs_ref[here, :].astype(F32)
        rms_inv = lax.rsqrt(jnp.mean(value * value, axis=-1, keepdims=True) + EPS)
        normed = value * rms_inv
        unit_grad = term_refs[0][here, :].astype(F32)
        for ref in term_refs[1:]:
            unit_grad = unit_grad + ref[here, :].astype(F32)
        scaled = unit_grad * gain_ref[...]
        mean = jnp.mean(scaled * normed, axis=-1, keepdims=True)
        result = grad_ref[here, :].astype(F32) + rms_inv * (scaled - normed * mean)
        out_ref[here, :] = result.astype(BF16)


def input_grad_of(inputs, gain, arriving, terms):
    rows, features = inputs.shape
    return pl.pallas_call(
        input_grad_kernel,
        out_shape=jax.ShapeDtypeStruct((rows, features), BF16),
        grid=(rows // 32,),
        in_specs=[row_blocks(32, features), pl.BlockSpec((1, features), lambda i: (0, 0))]
        + [row_blocks(32, features)] * (1 + len(terms)),
        out_specs=row_blocks(32, features),
        compiler_params=pltpu.CompilerParams(vmem_limit_bytes=ROOM),
        cost_estimate=SMALL,
    )(inputs, gain, arriving, *terms)


def body(
    inputs,
    norm_gain,
    incoming_grad,
    up_tiles,
    up_index,
    up_count,
    down_tiles,
    down_index,
    down_count,
):
    up, down = up_tiles[0], down_tiles[0]
    rows, features = inputs.shape[1:]
    count = up.shape[0]
    feature_blocks = features // SIDE
    unit_blocks = FF // lax.axis_size("tp") // SIDE
    by_unit = (count + unit_blocks * (PAIR - 1)) // PAIR
    by_feature = (count + feature_blocks * (PAIR - 1)) // PAIR
    width = rounded_up(PAIR * by_feature, SIDE)

    near, far = range(PIECES), range(PIECES, 2 * PIECES)

    units = {0: normed_units(inputs[0], norm_gain)}
    spread(units, (1, 2, 3))
    arriving = from_next_section(incoming_grad[0])
    lists = [
        group_lists(up_index[0], up_count[0, 0], 1, width),
        group_lists(down_index[0], down_count[0, 0], 0, width),
        group_lists(up_index[0], up_count[0, 0], 0, width),
    ]
    codes = jnp.stack([pair[0] for pair in lists])
    keys = jnp.stack([pair[1] for pair in lists])

    spread(units, (5, 4, 6), units[1], units[2], units[3])
    near_hidden, near_slope = hidden_of(
        codes, keys, [units[i] for i in near], up, unit_blocks, by_unit
    )
    last = (near_slope, units[4], units[5], units[6])
    spread(units, (7,), *last)
    grads = {0: after(arriving, *last)}
    spread(grads, (1, 2, 3))
    far_hidden, far_slope = hidden_of(
        codes, keys, [units[i] for i in far], up, unit_blocks, by_unit
    )
    spread(grads, (5, 4, 6), far_slope, grads[1], grads[2], grads[3])
    near_pre_grad = pre_grad_of(
        after(codes, far_slope), keys, [grads[i] for i in near], down, near_slope, by_unit
    )
    spread(grads, (7,), near_pre_grad)
    parts = unit_grad_of(
        after(codes, grads[4], grads[5], grads[6]), keys, near_pre_grad, up, rows, features, by_feature
    )
    terms = [parts[0]] + [returned(parts[i], i) for i in (1, 2, 3)]
    far_pre_grad = pre_grad_of(
        after(codes, *parts, grads[7]), keys, [grads[i] for i in far], down, far_slope, by_unit
    )
    parts += unit_grad_of(codes, keys, far_pre_grad, up, rows, features, by_feature)
    terms += [returned(after(parts[i], *terms[1:4]), i) for i in (7, 4, 5, 6)]
    pre_grads, hidden = [near_pre_grad, far_pre_grad], [near_hidden, far_hidden]
    up_grad = up_grad_of(
        after(codes, *parts), keys, [units[i] for i in range(2 * PIECES)], pre_grads, count, by_unit
    )
    down_grad = down_grad_of(
        after(codes, up_grad), keys, [grads[i] for i in range(2 * PIECES)], hidden, count, by_unit
    )
    input_grad = input_grad_of(inputs[0], norm_gain, arriving, terms)
    return (input_grad[None], up_grad[None], down_grad[None])


def solution(mesh):
    placed = (
        P("section", "tp", None),
        P("section", None),
        P("section", "tp", None),
        P("section", "tp", None, None),
        P("section", "tp", None),
        P("section", "tp"),
        P("section", "tp", None, None),
        P("section", "tp", None),
        P("section", "tp"),
    )
    return jax.shard_map(
        body,
        mesh=mesh,
        in_specs=placed,
        out_specs=(
            P("section", "tp", None),
            P("section", "tp", None, None),
            P("section", "tp", None, None),
        ),
        check_vma=False,
    )
```

```python
import functools

import jax
import jax.numpy as jnp
from jax import lax
from jax.experimental import pallas as pl
from jax.experimental.pallas import tpu as pltpu
from jax.sharding import PartitionSpec as P

FF = 14336
EPS = 1e-05
GELU_C = 0.7978845608028654
F32 = jnp.float32
BF16 = jnp.bfloat16
SIDE = 128
PAIR = 2
TREE = (
    (0, "y", "-"),
    (0, "+", "+"),
    (0, "-", "y"),
    (2, "+", "y"),
    (1, "-", "-"),
    (1, "+", "y"),
    (5, "-", "y"),
)
PIECES = 4
BACK = {"y": "y", "+": "-", "-": "+"}
ANY = pl.BlockSpec(memory_space=pl.ANY)
VMEM = pl.BlockSpec(memory_space=pltpu.VMEM)
SMEM = pl.BlockSpec(memory_space=pltpu.SMEM)
ROOM = 60 * 1024 * 1024
SMALL = pl.CostEstimate(flops=1024, bytes_accessed=1024, transcendentals=0)


def along(value, paths):
    sections, count = lax.axis_size("section"), lax.axis_size("tp")
    pairs = []
    for section in range(sections):
        for i in range(count):
            target = i
            for link in paths[section % 2]:
                target = target ^ 1 if link == "y" else (target + (2 if link == "+" else -2)) % count
            pairs.append((section * count + i, section * count + target))
    return lax.ppermute(value, ("section", "tp"), pairs)


def after(value, *earlier):
    return lax.optimization_barrier((value, *earlier))[0]


def from_next_section(value):
    count = lax.axis_size("section")
    return lax.ppermute(value, "section", [(i, (i - 1) % count) for i in range(count)])


def spread(pieces, steps, *earlier):
    for i in steps:
        parent, *links = TREE[i - 1]
        value = after(pieces[parent], *earlier) if earlier else pieces[parent]
        pieces[i] = along(value, links)


def returned(value, piece, until=0):
    paths = ["", ""]
    while piece != until:
        piece, *links = TREE[piece - 1]
        paths = [path + BACK[link] for path, link in zip(paths, links, strict=True)]
    return along(value, paths)


def lanes(block):
    return pl.ds(pl.multiple_of(block * SIDE, SIDE), SIDE)


def rounded_up(value, step):
    return -(-value // step) * step


def group_lists(index, count, key_column, width):
    length = index.shape[0]
    key, other = index[:, key_column], index[:, 1 - key_column]
    entry = jnp.arange(length, dtype=jnp.int32)
    live = entry < count
    same = (key[:, None] == key[None, :]) & live[None, :] & (entry[None, :] < entry[:, None])
    rank = jnp.sum(same.astype(jnp.int32), axis=1)
    opens = live & (rank % PAIR == 0)
    before = jnp.sum(((key[None, :] < key[:, None]) & opens[None, :]).astype(jnp.int32), axis=1)
    place = jnp.where(live, before * PAIR + rank, -1)
    at = jnp.arange(width, dtype=jnp.int32)
    empty = length * 32
    code = entry * 32 + other - empty
    codes = empty + jnp.sum(jnp.where(place[:, None] == at[None, :], code[:, None], 0), axis=0)
    keys = jnp.sum(jnp.where(place[:, None] == at[None, :] * PAIR, key[:, None], 0), axis=0)
    return codes, keys


def normed_kernel(inputs_ref, gain_ref, units_ref):
    for start in range(0, units_ref.shape[0], 16):
        at = pl.ds(start, 16)
        value = inputs_ref[at, :].astype(F32)
        rms_inv = lax.rsqrt(jnp.mean(value * value, axis=-1, keepdims=True) + EPS)
        units_ref[at, :] = (value * rms_inv * gain_ref[...]).astype(BF16)


def row_blocks(rows, features):
    return pl.BlockSpec((rows, features), lambda i: (i, 0))


def normed_units(inputs, gain):
    rows, features = inputs.shape
    return pl.pallas_call(
        normed_kernel,
        out_shape=jax.ShapeDtypeStruct((rows, features), BF16),
        grid=(rows // 32,),
        in_specs=[row_blocks(32, features), pl.BlockSpec((1, features), lambda i: (0, 0))],
        out_specs=row_blocks(32, features),
        compiler_params=pltpu.CompilerParams(vmem_limit_bytes=ROOM),
        cost_estimate=SMALL,
    )(inputs, gain)


def run_groups(count, unroll, one):
    whole = count // unroll

    @pl.loop(0, whole)
    def _(i):
        for j in range(unroll):
            one(i * unroll + j)

    for s in range(whole * unroll, count):
        one(s)


def start_tiles(tiles_ref, held, sem):
    count = tiles_ref.shape[0]
    copy = pltpu.make_async_copy(tiles_ref, held.at[pl.ds(0, count)], sem)
    copy.start()
    held[count] = jnp.zeros(held.shape[1:], BF16)
    return copy


def hidden_kernel(groups, codes_ref, keys_ref, *refs):
    unit_refs, (up_ref, hidden_ref, slope_ref, units, up, pre, sems) = refs[:PIECES], refs[PIECES:]
    rows = units.shape[0] // PIECES
    copies = [start_tiles(up_ref, up, sems.at[PIECES])]
    for i, ref in enumerate(unit_refs):
        copies.append(
            pltpu.make_async_copy(
                ref, units.at[pl.ds(i * rows, rows)], sems.at[i]
            )
        )
        copies[-1].start()
    pre[...] = jnp.zeros_like(pre)
    for copy in copies:
        copy.wait()

    def add(s):
        codes = [codes_ref[0, s * PAIR + i] for i in range(PAIR)]
        left = jnp.concatenate([units[:, lanes(code & 31)] for code in codes], axis=1)
        right = jnp.concatenate([up[code >> 5] for code in codes], axis=0)
        pre[:, lanes(keys_ref[0, s])] += jnp.dot(left, right, preferred_element_type=F32)

    run_groups(groups, 14, add)

    @pl.loop(0, pre.shape[0] // 32)
    def _(i):
        at = pl.ds(pl.multiple_of(i * 32, 32), 32)
        z = pre[at, :]
        square = z * z
        inner = jnp.tanh(GELU_C * (z + 0.044715 * square * z))
        hidden_ref[at, :] = (0.5 * z * (1.0 + inner)).astype(BF16)
        slope_ref[at, :] = 0.5 * (1.0 + inner) + 0.5 * z * (1.0 - inner * inner) * GELU_C * (
            1.0 + 3.0 * 0.044715 * square
        )


def hidden_of(codes, keys, units, up_tiles, unit_blocks, groups):
    rows, features = units[0].shape
    tokens, wide = PIECES * rows, unit_blocks * SIDE
    held = (up_tiles.shape[0] + 1,) + up_tiles.shape[1:]
    return pl.pallas_call(
        functools.partial(hidden_kernel, groups),
        out_shape=[
            jax.ShapeDtypeStruct((tokens, wide), BF16),
            jax.ShapeDtypeStruct((tokens, wide), F32),
        ],
        in_specs=[SMEM, SMEM] + [ANY] * (PIECES + 1),
        out_specs=[VMEM, VMEM],
        scratch_shapes=[
            pltpu.VMEM((tokens, features), BF16),
            pltpu.VMEM(held, BF16),
            pltpu.VMEM((tokens, wide), F32),
            pltpu.SemaphoreType.DMA((PIECES + 1,)),
        ],
        compiler_params=pltpu.CompilerParams(vmem_limit_bytes=ROOM),
        cost_estimate=SMALL,
    )(codes, keys, *units, up_tiles)


def pre_grad_kernel(pieces, start, groups, codes_ref, keys_ref, *refs):
    grad_refs, (down_ref, slope_ref, pre_grad_ref) = refs[:pieces], refs[pieces : pieces + 3]
    grads, down, slope, hidden_grad, sems = refs[pieces + 3 :]
    rows = grad_refs[0].shape[0]
    copies = [start_tiles(down_ref, down, sems.at[pieces])]
    for i, ref in enumerate(grad_refs):
        copies.append(
            pltpu.make_async_copy(ref, grads.at[pl.ds(i * rows, rows)], sems.at[i])
        )
        copies[-1].start()
    late = pltpu.make_async_copy(
        slope_ref.at[pl.ds(start, slope.shape[0])], slope, sems.at[pieces + 1]
    )
    late.start()
    hidden_grad[...] = jnp.zeros_like(hidden_grad)
    for copy in copies:
        copy.wait()

    def add(s):
        codes = [codes_ref[1, s * PAIR + i] for i in range(PAIR)]
        left = jnp.concatenate([grads[:, lanes(code & 31)] for code in codes], axis=1)
        right = jnp.concatenate([down[code >> 5] for code in codes], axis=1)
        hidden_grad[:, lanes(keys_ref[1, s])] += lax.dot_general(
            left, right, (((1,), (1,)), ((), ())), preferred_element_type=F32
        )

    run_groups(groups, 14, add)
    late.wait()

    @pl.loop(0, slope.shape[0] // 32)
    def _(i):
        at = pl.ds(pl.multiple_of(i * 32, 32), 32)
        pre_grad_ref[at, :] = (hidden_grad[at, :] * slope[at, :]).astype(BF16)


def pre_grad_of(codes, keys, grads, down_tiles, slope, groups, start=0):
    pieces = len(grads)
    rows, features = grads[0].shape
    tokens, wide = pieces * rows, slope.shape[1]
    held = (down_tiles.shape[0] + 1,) + down_tiles.shape[1:]
    return pl.pallas_call(
        functools.partial(pre_grad_kernel, pieces, start, groups),
        out_shape=jax.ShapeDtypeStruct((tokens, wide), BF16),
        in_specs=[SMEM, SMEM] + [ANY] * (pieces + 2),
        out_specs=VMEM,
        scratch_shapes=[
            pltpu.VMEM((tokens, features), BF16),
            pltpu.VMEM(held, BF16),
            pltpu.VMEM((tokens, wide), F32),
            pltpu.VMEM((tokens, wide), F32),
            pltpu.SemaphoreType.DMA((pieces + 2,)),
        ],
        compiler_params=pltpu.CompilerParams(vmem_limit_bytes=ROOM),
        cost_estimate=SMALL,
    )(codes, keys, *grads, down_tiles, slope)


def unit_grad_kernel(pieces, groups, codes_ref, keys_ref, pre_grad_ref, up_ref, *refs):
    out_refs, (up, total, sem) = refs[:pieces], refs[pieces:]
    rows = out_refs[0].shape[0]
    copy = start_tiles(up_ref, up, sem.at[0])
    total[...] = jnp.zeros_like(total)
    copy.wait()

    def add(s):
        codes = [codes_ref[2, s * PAIR + i] for i in range(PAIR)]
        left = jnp.concatenate([pre_grad_ref[:, lanes(code & 31)] for code in codes], axis=1)
        right = jnp.concatenate([up[code >> 5] for code in codes], axis=1)
        total[:, lanes(keys_ref[2, s])] += lax.dot_general(
            left, right, (((1,), (1,)), ((), ())), preferred_element_type=F32
        )

    run_groups(groups, 21, add)
    for piece, out_ref in enumerate(out_refs):

        @pl.loop(0, rows // 16)
        def _(i):
            step = pl.multiple_of(i * 16, 16)
            out_ref[pl.ds(step, 16), :] = total[pl.ds(piece * rows + step, 16), :].astype(BF16)


def unit_grad_of(codes, keys, pre_grad, up_tiles, rows, features, groups):
    tokens = pre_grad.shape[0]
    pieces = tokens // rows
    held = (up_tiles.shape[0] + 1,) + up_tiles.shape[1:]
    return pl.pallas_call(
        functools.partial(unit_grad_kernel, pieces, groups),
        out_shape=[jax.ShapeDtypeStruct((rows, features), BF16)] * pieces,
        in_specs=[SMEM, SMEM, VMEM, ANY],
        out_specs=[VMEM] * pieces,
        scratch_shapes=[
            pltpu.VMEM(held, BF16),
            pltpu.VMEM((tokens, features), F32),
            pltpu.SemaphoreType.DMA((1,)),
        ],
        compiler_params=pltpu.CompilerParams(vmem_limit_bytes=ROOM),
        cost_estimate=SMALL,
    )(codes, keys, pre_grad, up_tiles)


def up_grad_kernel(parts, groups, codes_ref, keys_ref, *refs):
    pieces = 2 * PIECES
    unit_refs, slope_refs = refs[:pieces], refs[pieces : pieces + parts]
    out_ref, units, slopes, held, sems = refs[pieces + parts :]
    rows, done = unit_refs[0].shape[0], 0
    copies = []
    for i, ref in enumerate(slope_refs):
        size = ref.shape[0]
        copies.append(
            pltpu.make_async_copy(ref, slopes.at[pl.ds(done, size)], sems.at[pieces + i])
        )
        done += size
    for i, ref in enumerate(unit_refs):
        copies.append(
            pltpu.make_async_copy(ref, units.at[pl.ds(i * rows, rows)], sems.at[i])
        )
    for copy in copies:
        copy.start()
    held[...] = jnp.zeros_like(held)
    for copy in copies:
        copy.wait()

    def one(s):
        codes = [codes_ref[0, s * PAIR + i] for i in range(PAIR)]
        left = jnp.concatenate([units[:, lanes(code & 31)] for code in codes], axis=1)
        summed = lax.dot_general(
            left,
            slopes[:, lanes(keys_ref[0, s])],
            (((0,), (0,)), ((), ())),
            preferred_element_type=F32,
        ).astype(BF16)
        for i, code in enumerate(codes):
            held[code >> 5] = summed[i * SIDE : (i + 1) * SIDE]

    run_groups(groups, 14, one)
    copy = pltpu.make_async_copy(held.at[pl.ds(0, out_ref.shape[0])], out_ref, sems.at[0])
    copy.start()
    copy.wait()


def up_grad_of(codes, keys, units, slopes, count, groups):
    pieces = len(units)
    rows, features = units[0].shape
    tokens, wide = pieces * rows, slopes[0].shape[1]
    return pl.pallas_call(
        functools.partial(up_grad_kernel, len(slopes), groups),
        out_shape=jax.ShapeDtypeStruct((count, SIDE, SIDE), BF16),
        in_specs=[SMEM, SMEM] + [ANY] * (pieces + len(slopes)),
        out_specs=ANY,
        scratch_shapes=[
            pltpu.VMEM((tokens, features), BF16),
            pltpu.VMEM((tokens, wide), BF16),
            pltpu.VMEM((count + 1, SIDE, SIDE), BF16),
            pltpu.SemaphoreType.DMA((pieces + len(slopes),)),
        ],
        compiler_params=pltpu.CompilerParams(vmem_limit_bytes=ROOM),
        cost_estimate=SMALL,
    )(codes, keys, *units, *slopes)


def down_grad_kernel(groups, codes_ref, keys_ref, *refs):
    pieces = 2 * PIECES
    grad_refs, hidden_refs = refs[:pieces], refs[pieces : pieces + 2]
    out_ref, grads, hidden, turned, held, sems = refs[pieces + 2 :]
    rows, half = grad_refs[0].shape[0], hidden_refs[0].shape[0]
    copies = []
    for i, ref in enumerate(hidden_refs):
        copies.append(pltpu.make_async_copy(ref, hidden.at[pl.ds(i * half, half)], sems.at[i]))
    late = []
    for i, ref in enumerate(grad_refs):
        late.append(
            pltpu.make_async_copy(ref, grads.at[pl.ds(i * rows, rows)], sems.at[2 + i])
        )
    for copy in copies + late:
        copy.start()
    held[...] = jnp.zeros_like(held)
    for copy in copies:
        copy.wait()

    @pl.loop(0, turned.shape[0])
    def _(c):
        turned[c] = hidden[:, lanes(c)].T

    for copy in late:
        copy.wait()

    def one(s):
        codes = [codes_ref[1, s * PAIR + i] for i in range(PAIR)]
        right = jnp.concatenate([grads[:, lanes(code & 31)] for code in codes], axis=1)
        summed = jnp.dot(turned[keys_ref[1, s]], right, preferred_element_type=F32).astype(BF16)
        for i, code in enumerate(codes):
            held[code >> 5] = summed[:, i * SIDE : (i + 1) * SIDE]

    run_groups(groups, 14, one)
    copy = pltpu.make_async_copy(held.at[pl.ds(0, out_ref.shape[0])], out_ref, sems.at[0])
    copy.start()
    copy.wait()


def down_grad_of(codes, keys, grads, hidden, count, groups):
    pieces = len(grads)
    rows, features = grads[0].shape
    tokens, wide = pieces * rows, hidden[0].shape[1]
    return pl.pallas_call(
        functools.partial(down_grad_kernel, groups),
        out_shape=jax.ShapeDtypeStruct((count, SIDE, SIDE), BF16),
        in_specs=[SMEM, SMEM] + [ANY] * (pieces + 2),
        out_specs=ANY,
        scratch_shapes=[
            pltpu.VMEM((tokens, features), BF16),
            pltpu.VMEM((tokens, wide), BF16),
            pltpu.VMEM((wide // SIDE, SIDE, tokens), BF16),
            pltpu.VMEM((count + 1, SIDE, SIDE), BF16),
            pltpu.SemaphoreType.DMA((2 + pieces,)),
        ],
        compiler_params=pltpu.CompilerParams(vmem_limit_bytes=ROOM),
        cost_estimate=SMALL,
    )(codes, keys, *grads, *hidden)


def input_grad_kernel(inputs_ref, gain_ref, grad_ref, *refs):
    term_refs, out_ref = refs[:-1], refs[-1]
    for start in range(0, out_ref.shape[0], 16):
        here = pl.ds(start, 16)
        value = inputs_ref[here, :].astype(F32)
        rms_inv = lax.rsqrt(jnp.mean(value * value, axis=-1, keepdims=True) + EPS)
        normed = value * rms_inv
        unit_grad = term_refs[0][here, :].astype(F32)
        for ref in term_refs[1:]:
            unit_grad = unit_grad + ref[here, :].astype(F32)
        scaled = unit_grad * gain_ref[...]
        mean = jnp.mean(scaled * normed, axis=-1, keepdims=True)
        result = grad_ref[here, :].astype(F32) + rms_inv * (scaled - normed * mean)
        out_ref[here, :] = result.astype(BF16)


def input_grad_of(inputs, gain, arriving, terms):
    rows, features = inputs.shape
    return pl.pallas_call(
        input_grad_kernel,
        out_shape=jax.ShapeDtypeStruct((rows, features), BF16),
        grid=(rows // 32,),
        in_specs=[row_blocks(32, features), pl.BlockSpec((1, features), lambda i: (0, 0))]
        + [row_blocks(32, features)] * (1 + len(terms)),
        out_specs=row_blocks(32, features),
        compiler_params=pltpu.CompilerParams(vmem_limit_bytes=ROOM),
        cost_estimate=SMALL,
    )(inputs, gain, arriving, *terms)


def body(
    inputs,
    norm_gain,
    incoming_grad,
    up_tiles,
    up_index,
    up_count,
    down_tiles,
    down_index,
    down_count,
):
    up, down = up_tiles[0], down_tiles[0]
    rows, features = inputs.shape[1:]
    count = up.shape[0]
    feature_blocks = features // SIDE
    unit_blocks = FF // lax.axis_size("tp") // SIDE
    by_unit = (count + unit_blocks * (PAIR - 1)) // PAIR
    by_feature = (count + feature_blocks * (PAIR - 1)) // PAIR
    width = rounded_up(PAIR * by_feature, SIDE)

    near, far = range(PIECES), range(PIECES, 2 * PIECES)

    units = {0: normed_units(inputs[0], norm_gain)}
    spread(units, (1, 2, 3))
    arriving = from_next_section(incoming_grad[0])
    lists = [
        group_lists(up_index[0], up_count[0, 0], 1, width),
        group_lists(down_index[0], down_count[0, 0], 0, width),
        group_lists(up_index[0], up_count[0, 0], 0, width),
    ]
    codes = jnp.stack([pair[0] for pair in lists])
    keys = jnp.stack([pair[1] for pair in lists])

    spread(units, (5, 4, 6), units[1], units[2], units[3])
    near_hidden, near_slope = hidden_of(
        codes, keys, [units[i] for i in near], up, unit_blocks, by_unit
    )
    last = (near_slope, units[4], units[5], units[6])
    spread(units, (7,), *last)
    grads = {0: after(arriving, *last)}
    spread(grads, (1, 2, 3))
    far_hidden, far_slope = hidden_of(
        codes, keys, [units[i] for i in far], up, unit_blocks, by_unit
    )
    spread(grads, (5, 4, 6), far_slope, grads[1], grads[2], grads[3])
    near_pre_grad = pre_grad_of(
        after(codes, far_slope), keys, [grads[i] for i in near], down, near_slope, by_unit
    )
    spread(grads, (7,), near_pre_grad)
    parts = unit_grad_of(
        after(codes, grads[4], grads[5]), keys, near_pre_grad, up, rows, features, by_feature
    )
    terms = [parts[0]] + [returned(after(parts[i], grads[6]), i) for i in (1, 2, 3)]
    far_pre_grad = pre_grad_of(
        after(codes, *parts, grads[7]), keys, [grads[i] for i in far], down, far_slope, by_unit
    )
    parts += unit_grad_of(codes, keys, far_pre_grad, up, rows, features, by_feature)
    terms += [returned(after(parts[i], *terms[1:4]), i) for i in (7, 4, 5, 6)]
    pre_grads, hidden = [near_pre_grad, far_pre_grad], [near_hidden, far_hidden]
    up_grad = up_grad_of(
        after(codes, *parts), keys, [units[i] for i in range(2 * PIECES)], pre_grads, count, by_unit
    )
    down_grad = down_grad_of(
        after(codes, up_grad), keys, [grads[i] for i in range(2 * PIECES)], hidden, count, by_unit
    )
    input_grad = input_grad_of(inputs[0], norm_gain, arriving, terms)
    return (input_grad[None], up_grad[None], down_grad[None])


def solution(mesh):
    placed = (
        P("section", "tp", None),
        P("section", None),
        P("section", "tp", None),
        P("section", "tp", None, None),
        P("section", "tp", None),
        P("section", "tp"),
        P("section", "tp", None, None),
        P("section", "tp", None),
        P("section", "tp"),
    )
    return jax.shard_map(
        body,
        mesh=mesh,
        in_specs=placed,
        out_specs=(
            P("section", "tp", None),
            P("section", "tp", None, None),
            P("section", "tp", None, None),
        ),
        check_vma=False,
    )
```

```python
import functools

import jax
import jax.numpy as jnp
from jax import lax
from jax.experimental import pallas as pl
from jax.experimental.pallas import tpu as pltpu
from jax.sharding import PartitionSpec as P

FF = 14336
EPS = 1e-05
GELU_C = 0.7978845608028654
F32 = jnp.float32
BF16 = jnp.bfloat16
SIDE = 128
PAIR = 2
TREE = (
    (0, "y", "-"),
    (0, "+", "+"),
    (0, "-", "y"),
    (2, "+", "y"),
    (1, "-", "-"),
    (1, "+", "y"),
    (5, "-", "y"),
)
PIECES = 4
BACK = {"y": "y", "+": "-", "-": "+"}
ANY = pl.BlockSpec(memory_space=pl.ANY)
VMEM = pl.BlockSpec(memory_space=pltpu.VMEM)
SMEM = pl.BlockSpec(memory_space=pltpu.SMEM)
ROOM = 60 * 1024 * 1024
SMALL = pl.CostEstimate(flops=1024, bytes_accessed=1024, transcendentals=0)


def along(value, paths):
    sections, count = lax.axis_size("section"), lax.axis_size("tp")
    pairs = []
    for section in range(sections):
        for i in range(count):
            target = i
            for link in paths[section % 2]:
                target = target ^ 1 if link == "y" else (target + (2 if link == "+" else -2)) % count
            pairs.append((section * count + i, section * count + target))
    return lax.ppermute(value, ("section", "tp"), pairs)


def after(value, *earlier):
    return lax.optimization_barrier((value, *earlier))[0]


def from_next_section(value):
    count = lax.axis_size("section")
    return lax.ppermute(value, "section", [(i, (i - 1) % count) for i in range(count)])


def spread(pieces, steps, *earlier):
    for i in steps:
        parent, *links = TREE[i - 1]
        value = after(pieces[parent], *earlier) if earlier else pieces[parent]
        pieces[i] = along(value, links)


def returned(value, piece, until=0):
    paths = ["", ""]
    while piece != until:
        piece, *links = TREE[piece - 1]
        paths = [path + BACK[link] for path, link in zip(paths, links, strict=True)]
    return along(value, paths)


def lanes(block):
    return pl.ds(pl.multiple_of(block * SIDE, SIDE), SIDE)


def rounded_up(value, step):
    return -(-value // step) * step


def group_lists(index, count, key_column, width):
    length = index.shape[0]
    key, other = index[:, key_column], index[:, 1 - key_column]
    entry = jnp.arange(length, dtype=jnp.int32)
    live = entry < count
    same = (key[:, None] == key[None, :]) & live[None, :] & (entry[None, :] < entry[:, None])
    rank = jnp.sum(same.astype(jnp.int32), axis=1)
    opens = live & (rank % PAIR == 0)
    before = jnp.sum(((key[None, :] < key[:, None]) & opens[None, :]).astype(jnp.int32), axis=1)
    place = jnp.where(live, before * PAIR + rank, -1)
    at = jnp.arange(width, dtype=jnp.int32)
    empty = length * 32
    code = entry * 32 + other - empty
    codes = empty + jnp.sum(jnp.where(place[:, None] == at[None, :], code[:, None], 0), axis=0)
    keys = jnp.sum(jnp.where(place[:, None] == at[None, :] * PAIR, key[:, None], 0), axis=0)
    return codes, keys


def normed_kernel(inputs_ref, gain_ref, units_ref):
    for start in range(0, units_ref.shape[0], 16):
        at = pl.ds(start, 16)
        value = inputs_ref[at, :].astype(F32)
        rms_inv = lax.rsqrt(jnp.mean(value * value, axis=-1, keepdims=True) + EPS)
        units_ref[at, :] = (value * rms_inv * gain_ref[...]).astype(BF16)


def row_blocks(rows, features):
    return pl.BlockSpec((rows, features), lambda i: (i, 0))


def normed_units(inputs, gain):
    rows, features = inputs.shape
    return pl.pallas_call(
        normed_kernel,
        out_shape=jax.ShapeDtypeStruct((rows, features), BF16),
        grid=(rows // 32,),
        in_specs=[row_blocks(32, features), pl.BlockSpec((1, features), lambda i: (0, 0))],
        out_specs=row_blocks(32, features),
        compiler_params=pltpu.CompilerParams(vmem_limit_bytes=ROOM),
        cost_estimate=SMALL,
    )(inputs, gain)


def run_groups(count, unroll, one):
    whole = count // unroll

    @pl.loop(0, whole)
    def _(i):
        for j in range(unroll):
            one(i * unroll + j)

    for s in range(whole * unroll, count):
        one(s)


def start_tiles(tiles_ref, held, sem):
    count = tiles_ref.shape[0]
    copy = pltpu.make_async_copy(tiles_ref, held.at[pl.ds(0, count)], sem)
    copy.start()
    held[count] = jnp.zeros(held.shape[1:], BF16)
    return copy


def hidden_kernel(groups, codes_ref, keys_ref, *refs):
    unit_refs, (up_ref, hidden_ref, slope_ref, units, up, pre, sems) = refs[:PIECES], refs[PIECES:]
    rows = units.shape[0] // PIECES
    copies = [start_tiles(up_ref, up, sems.at[PIECES])]
    for i, ref in enumerate(unit_refs):
        copies.append(
            pltpu.make_async_copy(
                ref, units.at[pl.ds(i * rows, rows)], sems.at[i]
            )
        )
        copies[-1].start()
    pre[...] = jnp.zeros_like(pre)
    for copy in copies:
        copy.wait()

    def add(s):
        codes = [codes_ref[0, s * PAIR + i] for i in range(PAIR)]
        left = jnp.concatenate([units[:, lanes(code & 31)] for code in codes], axis=1)
        right = jnp.concatenate([up[code >> 5] for code in codes], axis=0)
        pre[:, lanes(keys_ref[0, s])] += jnp.dot(left, right, preferred_element_type=F32)

    run_groups(groups, 14, add)

    @pl.loop(0, pre.shape[0] // 32)
    def _(i):
        at = pl.ds(pl.multiple_of(i * 32, 32), 32)
        z = pre[at, :]
        square = z * z
        inner = jnp.tanh(GELU_C * (z + 0.044715 * square * z))
        hidden_ref[at, :] = (0.5 * z * (1.0 + inner)).astype(BF16)
        slope_ref[at, :] = 0.5 * (1.0 + inner) + 0.5 * z * (1.0 - inner * inner) * GELU_C * (
            1.0 + 3.0 * 0.044715 * square
        )


def hidden_of(codes, keys, units, up_tiles, unit_blocks, groups):
    rows, features = units[0].shape
    tokens, wide = PIECES * rows, unit_blocks * SIDE
    held = (up_tiles.shape[0] + 1,) + up_tiles.shape[1:]
    return pl.pallas_call(
        functools.partial(hidden_kernel, groups),
        out_shape=[
            jax.ShapeDtypeStruct((tokens, wide), BF16),
            jax.ShapeDtypeStruct((tokens, wide), F32),
        ],
        in_specs=[SMEM, SMEM] + [ANY] * (PIECES + 1),
        out_specs=[VMEM, VMEM],
        scratch_shapes=[
            pltpu.VMEM((tokens, features), BF16),
            pltpu.VMEM(held, BF16),
            pltpu.VMEM((tokens, wide), F32),
            pltpu.SemaphoreType.DMA((PIECES + 1,)),
        ],
        compiler_params=pltpu.CompilerParams(vmem_limit_bytes=ROOM),
        cost_estimate=SMALL,
    )(codes, keys, *units, up_tiles)


def pre_grad_kernel(pieces, start, groups, codes_ref, keys_ref, *refs):
    grad_refs, (down_ref, slope_ref, pre_grad_ref) = refs[:pieces], refs[pieces : pieces + 3]
    grads, down, slope, hidden_grad, sems = refs[pieces + 3 :]
    rows = grad_refs[0].shape[0]
    copies = [start_tiles(down_ref, down, sems.at[pieces])]
    for i, ref in enumerate(grad_refs):
        copies.append(
            pltpu.make_async_copy(ref, grads.at[pl.ds(i * rows, rows)], sems.at[i])
        )
        copies[-1].start()
    late = pltpu.make_async_copy(
        slope_ref.at[pl.ds(start, slope.shape[0])], slope, sems.at[pieces + 1]
    )
    late.start()
    hidden_grad[...] = jnp.zeros_like(hidden_grad)
    for copy in copies:
        copy.wait()

    def add(s):
        codes = [codes_ref[1, s * PAIR + i] for i in range(PAIR)]
        left = jnp.concatenate([grads[:, lanes(code & 31)] for code in codes], axis=1)
        right = jnp.concatenate([down[code >> 5] for code in codes], axis=1)
        hidden_grad[:, lanes(keys_ref[1, s])] += lax.dot_general(
            left, right, (((1,), (1,)), ((), ())), preferred_element_type=F32
        )

    run_groups(groups, 14, add)
    late.wait()

    @pl.loop(0, slope.shape[0] // 32)
    def _(i):
        at = pl.ds(pl.multiple_of(i * 32, 32), 32)
        pre_grad_ref[at, :] = (hidden_grad[at, :] * slope[at, :]).astype(BF16)


def pre_grad_of(codes, keys, grads, down_tiles, slope, groups, start=0):
    pieces = len(grads)
    rows, features = grads[0].shape
    tokens, wide = pieces * rows, slope.shape[1]
    held = (down_tiles.shape[0] + 1,) + down_tiles.shape[1:]
    return pl.pallas_call(
        functools.partial(pre_grad_kernel, pieces, start, groups),
        out_shape=jax.ShapeDtypeStruct((tokens, wide), BF16),
        in_specs=[SMEM, SMEM] + [ANY] * (pieces + 2),
        out_specs=VMEM,
        scratch_shapes=[
            pltpu.VMEM((tokens, features), BF16),
            pltpu.VMEM(held, BF16),
            pltpu.VMEM((tokens, wide), F32),
            pltpu.VMEM((tokens, wide), F32),
            pltpu.SemaphoreType.DMA((pieces + 2,)),
        ],
        compiler_params=pltpu.CompilerParams(vmem_limit_bytes=ROOM),
        cost_estimate=SMALL,
    )(codes, keys, *grads, down_tiles, slope)


def unit_grad_kernel(pieces, groups, codes_ref, keys_ref, pre_grad_ref, up_ref, *refs):
    out_refs, (up, total, sem) = refs[:pieces], refs[pieces:]
    rows = out_refs[0].shape[0]
    copy = start_tiles(up_ref, up, sem.at[0])
    total[...] = jnp.zeros_like(total)
    copy.wait()

    def add(s):
        codes = [codes_ref[2, s * PAIR + i] for i in range(PAIR)]
        left = jnp.concatenate([pre_grad_ref[:, lanes(code & 31)] for code in codes], axis=1)
        right = jnp.concatenate([up[code >> 5] for code in codes], axis=1)
        total[:, lanes(keys_ref[2, s])] += lax.dot_general(
            left, right, (((1,), (1,)), ((), ())), preferred_element_type=F32
        )

    run_groups(groups, 21, add)
    for piece, out_ref in enumerate(out_refs):

        @pl.loop(0, rows // 16)
        def _(i):
            step = pl.multiple_of(i * 16, 16)
            out_ref[pl.ds(step, 16), :] = total[pl.ds(piece * rows + step, 16), :].astype(BF16)


def unit_grad_of(codes, keys, pre_grad, up_tiles, rows, features, groups):
    tokens = pre_grad.shape[0]
    pieces = tokens // rows
    held = (up_tiles.shape[0] + 1,) + up_tiles.shape[1:]
    return pl.pallas_call(
        functools.partial(unit_grad_kernel, pieces, groups),
        out_shape=[jax.ShapeDtypeStruct((rows, features), BF16)] * pieces,
        in_specs=[SMEM, SMEM, VMEM, ANY],
        out_specs=[VMEM] * pieces,
        scratch_shapes=[
            pltpu.VMEM(held, BF16),
            pltpu.VMEM((tokens, features), F32),
            pltpu.SemaphoreType.DMA((1,)),
        ],
        compiler_params=pltpu.CompilerParams(vmem_limit_bytes=ROOM),
        cost_estimate=SMALL,
    )(codes, keys, pre_grad, up_tiles)


def both_grads_kernel(pieces, by_unit, by_feature, codes_ref, keys_ref, *refs):
    grad_refs, (down_ref, slope_ref, up_ref, pre_grad_ref) = refs[:pieces], refs[pieces : pieces + 4]
    out_refs = refs[pieces + 4 : 2 * pieces + 4]
    grads, down, slope, hidden_grad, up, total, sems = refs[2 * pieces + 4 :]
    rows = grad_refs[0].shape[0]
    copies = [start_tiles(down_ref, down, sems.at[pieces])]
    for i, ref in enumerate(grad_refs):
        copies.append(
            pltpu.make_async_copy(ref, grads.at[pl.ds(i * rows, rows)], sems.at[i])
        )
        copies[-1].start()
    slope_copy = pltpu.make_async_copy(slope_ref, slope, sems.at[pieces + 1])
    slope_copy.start()
    up_copy = start_tiles(up_ref, up, sems.at[pieces + 2])
    hidden_grad[...] = jnp.zeros_like(hidden_grad)
    total[...] = jnp.zeros_like(total)
    for copy in copies:
        copy.wait()

    def add_hidden_grad(s):
        codes = [codes_ref[1, s * PAIR + i] for i in range(PAIR)]
        left = jnp.concatenate([grads[:, lanes(code & 31)] for code in codes], axis=1)
        right = jnp.concatenate([down[code >> 5] for code in codes], axis=1)
        hidden_grad[:, lanes(keys_ref[1, s])] += lax.dot_general(
            left, right, (((1,), (1,)), ((), ())), preferred_element_type=F32
        )

    run_groups(by_unit, 14, add_hidden_grad)
    slope_copy.wait()

    @pl.loop(0, slope.shape[0] // 32)
    def _(i):
        at = pl.ds(pl.multiple_of(i * 32, 32), 32)
        pre_grad_ref[at, :] = (hidden_grad[at, :] * slope[at, :]).astype(BF16)

    up_copy.wait()

    def add_unit_grad(s):
        codes = [codes_ref[2, s * PAIR + i] for i in range(PAIR)]
        left = jnp.concatenate([pre_grad_ref[:, lanes(code & 31)] for code in codes], axis=1)
        right = jnp.concatenate([up[code >> 5] for code in codes], axis=1)
        total[:, lanes(keys_ref[2, s])] += lax.dot_general(
            left, right, (((1,), (1,)), ((), ())), preferred_element_type=F32
        )

    run_groups(by_feature, 21, add_unit_grad)
    for piece, out_ref in enumerate(out_refs):

        @pl.loop(0, rows // 16)
        def _(i):
            step = pl.multiple_of(i * 16, 16)
            out_ref[pl.ds(step, 16), :] = total[pl.ds(piece * rows + step, 16), :].astype(BF16)


def both_grads_of(codes, keys, grads, down_tiles, slope, up_tiles, by_unit, by_feature):
    pieces = len(grads)
    rows, features = grads[0].shape
    tokens, wide = slope.shape
    held = (up_tiles.shape[0] + 1,) + up_tiles.shape[1:]
    pre_grad, *parts = pl.pallas_call(
        functools.partial(both_grads_kernel, pieces, by_unit, by_feature),
        out_shape=[jax.ShapeDtypeStruct((tokens, wide), BF16)]
        + [jax.ShapeDtypeStruct((rows, features), BF16)] * pieces,
        in_specs=[SMEM, SMEM] + [ANY] * (pieces + 3),
        out_specs=[VMEM] * (1 + pieces),
        scratch_shapes=[
            pltpu.VMEM((tokens, features), BF16),
            pltpu.VMEM(held, BF16),
            pltpu.VMEM((tokens, wide), F32),
            pltpu.VMEM((tokens, wide), F32),
            pltpu.VMEM(held, BF16),
            pltpu.VMEM((tokens, features), F32),
            pltpu.SemaphoreType.DMA((pieces + 3,)),
        ],
        compiler_params=pltpu.CompilerParams(vmem_limit_bytes=ROOM),
        cost_estimate=SMALL,
    )(codes, keys, *grads, down_tiles, slope, up_tiles)
    return pre_grad, parts


def up_grad_kernel(parts, groups, codes_ref, keys_ref, *refs):
    pieces = 2 * PIECES
    unit_refs, slope_refs = refs[:pieces], refs[pieces : pieces + parts]
    out_ref, units, slopes, held, sems = refs[pieces + parts :]
    rows, done = unit_refs[0].shape[0], 0
    copies = []
    for i, ref in enumerate(slope_refs):
        size = ref.shape[0]
        copies.append(
            pltpu.make_async_copy(ref, slopes.at[pl.ds(done, size)], sems.at[pieces + i])
        )
        done += size
    for i, ref in enumerate(unit_refs):
        copies.append(
            pltpu.make_async_copy(ref, units.at[pl.ds(i * rows, rows)], sems.at[i])
        )
    for copy in copies:
        copy.start()
    held[...] = jnp.zeros_like(held)
    for copy in copies:
        copy.wait()

    def one(s):
        codes = [codes_ref[0, s * PAIR + i] for i in range(PAIR)]
        left = jnp.concatenate([units[:, lanes(code & 31)] for code in codes], axis=1)
        summed = lax.dot_general(
            left,
            slopes[:, lanes(keys_ref[0, s])],
            (((0,), (0,)), ((), ())),
            preferred_element_type=F32,
        ).astype(BF16)
        for i, code in enumerate(codes):
            held[code >> 5] = summed[i * SIDE : (i + 1) * SIDE]

    run_groups(groups, 14, one)
    copy = pltpu.make_async_copy(held.at[pl.ds(0, out_ref.shape[0])], out_ref, sems.at[0])
    copy.start()
    copy.wait()


def up_grad_of(codes, keys, units, slopes, count, groups):
    pieces = len(units)
    rows, features = units[0].shape
    tokens, wide = pieces * rows, slopes[0].shape[1]
    return pl.pallas_call(
        functools.partial(up_grad_kernel, len(slopes), groups),
        out_shape=jax.ShapeDtypeStruct((count, SIDE, SIDE), BF16),
        in_specs=[SMEM, SMEM] + [ANY] * (pieces + len(slopes)),
        out_specs=ANY,
        scratch_shapes=[
            pltpu.VMEM((tokens, features), BF16),
            pltpu.VMEM((tokens, wide), BF16),
            pltpu.VMEM((count + 1, SIDE, SIDE), BF16),
            pltpu.SemaphoreType.DMA((pieces + len(slopes),)),
        ],
        compiler_params=pltpu.CompilerParams(vmem_limit_bytes=ROOM),
        cost_estimate=SMALL,
    )(codes, keys, *units, *slopes)


def down_grad_kernel(groups, codes_ref, keys_ref, *refs):
    pieces = 2 * PIECES
    grad_refs, hidden_refs = refs[:pieces], refs[pieces : pieces + 2]
    out_ref, grads, hidden, turned, held, sems = refs[pieces + 2 :]
    rows, half = grad_refs[0].shape[0], hidden_refs[0].shape[0]
    copies = []
    for i, ref in enumerate(hidden_refs):
        copies.append(pltpu.make_async_copy(ref, hidden.at[pl.ds(i * half, half)], sems.at[i]))
    late = []
    for i, ref in enumerate(grad_refs):
        late.append(
            pltpu.make_async_copy(ref, grads.at[pl.ds(i * rows, rows)], sems.at[2 + i])
        )
    for copy in copies + late:
        copy.start()
    held[...] = jnp.zeros_like(held)
    for copy in copies:
        copy.wait()

    @pl.loop(0, turned.shape[0])
    def _(c):
        turned[c] = hidden[:, lanes(c)].T

    for copy in late:
        copy.wait()

    def one(s):
        codes = [codes_ref[1, s * PAIR + i] for i in range(PAIR)]
        right = jnp.concatenate([grads[:, lanes(code & 31)] for code in codes], axis=1)
        summed = jnp.dot(turned[keys_ref[1, s]], right, preferred_element_type=F32).astype(BF16)
        for i, code in enumerate(codes):
            held[code >> 5] = summed[:, i * SIDE : (i + 1) * SIDE]

    run_groups(groups, 14, one)
    copy = pltpu.make_async_copy(held.at[pl.ds(0, out_ref.shape[0])], out_ref, sems.at[0])
    copy.start()
    copy.wait()


def down_grad_of(codes, keys, grads, hidden, count, groups):
    pieces = len(grads)
    rows, features = grads[0].shape
    tokens, wide = pieces * rows, hidden[0].shape[1]
    return pl.pallas_call(
        functools.partial(down_grad_kernel, groups),
        out_shape=jax.ShapeDtypeStruct((count, SIDE, SIDE), BF16),
        in_specs=[SMEM, SMEM] + [ANY] * (pieces + 2),
        out_specs=ANY,
        scratch_shapes=[
            pltpu.VMEM((tokens, features), BF16),
            pltpu.VMEM((tokens, wide), BF16),
            pltpu.VMEM((wide // SIDE, SIDE, tokens), BF16),
            pltpu.VMEM((count + 1, SIDE, SIDE), BF16),
            pltpu.SemaphoreType.DMA((2 + pieces,)),
        ],
        compiler_params=pltpu.CompilerParams(vmem_limit_bytes=ROOM),
        cost_estimate=SMALL,
    )(codes, keys, *grads, *hidden)


def input_grad_kernel(inputs_ref, gain_ref, grad_ref, *refs):
    term_refs, out_ref = refs[:-1], refs[-1]
    for start in range(0, out_ref.shape[0], 16):
        here = pl.ds(start, 16)
        value = inputs_ref[here, :].astype(F32)
        rms_inv = lax.rsqrt(jnp.mean(value * value, axis=-1, keepdims=True) + EPS)
        normed = value * rms_inv
        unit_grad = term_refs[0][here, :].astype(F32)
        for ref in term_refs[1:]:
            unit_grad = unit_grad + ref[here, :].astype(F32)
        scaled = unit_grad * gain_ref[...]
        mean = jnp.mean(scaled * normed, axis=-1, keepdims=True)
        result = grad_ref[here, :].astype(F32) + rms_inv * (scaled - normed * mean)
        out_ref[here, :] = result.astype(BF16)


def input_grad_of(inputs, gain, arriving, terms):
    rows, features = inputs.shape
    return pl.pallas_call(
        input_grad_kernel,
        out_shape=jax.ShapeDtypeStruct((rows, features), BF16),
        grid=(rows // 32,),
        in_specs=[row_blocks(32, features), pl.BlockSpec((1, features), lambda i: (0, 0))]
        + [row_blocks(32, features)] * (1 + len(terms)),
        out_specs=row_blocks(32, features),
        compiler_params=pltpu.CompilerParams(vmem_limit_bytes=ROOM),
        cost_estimate=SMALL,
    )(inputs, gain, arriving, *terms)


def body(
    inputs,
    norm_gain,
    incoming_grad,
    up_tiles,
    up_index,
    up_count,
    down_tiles,
    down_index,
    down_count,
):
    up, down = up_tiles[0], down_tiles[0]
    rows, features = inputs.shape[1:]
    count = up.shape[0]
    feature_blocks = features // SIDE
    unit_blocks = FF // lax.axis_size("tp") // SIDE
    by_unit = (count + unit_blocks * (PAIR - 1)) // PAIR
    by_feature = (count + feature_blocks * (PAIR - 1)) // PAIR
    width = rounded_up(PAIR * by_feature, SIDE)

    near, far = range(PIECES), range(PIECES, 2 * PIECES)

    units = {0: normed_units(inputs[0], norm_gain)}
    spread(units, (1, 2, 3))
    arriving = from_next_section(incoming_grad[0])
    lists = [
        group_lists(up_index[0], up_count[0, 0], 1, width),
        group_lists(down_index[0], down_count[0, 0], 0, width),
        group_lists(up_index[0], up_count[0, 0], 0, width),
    ]
    codes = jnp.stack([pair[0] for pair in lists])
    keys = jnp.stack([pair[1] for pair in lists])

    spread(units, (5, 4, 6), units[1], units[2], units[3])
    near_hidden, near_slope = hidden_of(
        codes, keys, [units[i] for i in near], up, unit_blocks, by_unit
    )
    last = (near_slope, units[4], units[5], units[6])
    spread(units, (7,), *last)
    grads = {0: after(arriving, *last)}
    spread(grads, (1, 2, 3))
    far_hidden, far_slope = hidden_of(
        codes, keys, [units[i] for i in far], up, unit_blocks, by_unit
    )
    spread(grads, (5, 4, 6), far_slope, grads[1], grads[2], grads[3])
    near_pre_grad = pre_grad_of(
        after(codes, far_slope), keys, [grads[i] for i in near], down, near_slope, by_unit
    )
    spread(grads, (7,), near_pre_grad)
    parts = unit_grad_of(
        after(codes, grads[4], grads[5]), keys, near_pre_grad, up, rows, features, by_feature
    )
    terms = [parts[0]] + [returned(after(parts[i], grads[6]), i) for i in (1, 2, 3)]
    far_pre_grad, far_parts = both_grads_of(
        after(codes, *parts, grads[7]),
        keys,
        [grads[i] for i in far],
        down,
        far_slope,
        up,
        by_unit,
        by_feature,
    )
    parts = [*parts, *far_parts]
    terms += [returned(after(parts[i], *terms[1:4]), i) for i in (7, 4, 5, 6)]
    pre_grads, hidden = [near_pre_grad, far_pre_grad], [near_hidden, far_hidden]
    up_grad = up_grad_of(
        after(codes, *parts), keys, [units[i] for i in range(2 * PIECES)], pre_grads, count, by_unit
    )
    down_grad = down_grad_of(
        after(codes, up_grad), keys, [grads[i] for i in range(2 * PIECES)], hidden, count, by_unit
    )
    input_grad = input_grad_of(inputs[0], norm_gain, arriving, terms)
    return (input_grad[None], up_grad[None], down_grad[None])


def solution(mesh):
    placed = (
        P("section", "tp", None),
        P("section", None),
        P("section", "tp", None),
        P("section", "tp", None, None),
        P("section", "tp", None),
        P("section", "tp"),
        P("section", "tp", None, None),
        P("section", "tp", None),
        P("section", "tp"),
    )
    return jax.shard_map(
        body,
        mesh=mesh,
        in_specs=placed,
        out_specs=(
            P("section", "tp", None),
            P("section", "tp", None, None),
            P("section", "tp", None, None),
        ),
        check_vma=False,
    )
```

```python
import functools

import jax
import jax.numpy as jnp
from jax import lax
from jax.experimental import pallas as pl
from jax.experimental.pallas import tpu as pltpu
from jax.sharding import PartitionSpec as P

FF = 14336
EPS = 1e-05
GELU_C = 0.7978845608028654
F32 = jnp.float32
BF16 = jnp.bfloat16
SIDE = 128
PAIR = 2
TREE = (
    (0, "y", "-"),
    (0, "+", "+"),
    (0, "-", "y"),
    (2, "+", "y"),
    (1, "-", "-"),
    (1, "+", "y"),
    (5, "-", "y"),
)
PIECES = 4
BACK = {"y": "y", "+": "-", "-": "+"}
ANY = pl.BlockSpec(memory_space=pl.ANY)
VMEM = pl.BlockSpec(memory_space=pltpu.VMEM)
SMEM = pl.BlockSpec(memory_space=pltpu.SMEM)
ROOM = 60 * 1024 * 1024
SMALL = pl.CostEstimate(flops=1024, bytes_accessed=1024, transcendentals=0)


def along(value, paths):
    sections, count = lax.axis_size("section"), lax.axis_size("tp")
    pairs = []
    for section in range(sections):
        for i in range(count):
            target = i
            for link in paths[section % 2]:
                target = target ^ 1 if link == "y" else (target + (2 if link == "+" else -2)) % count
            pairs.append((section * count + i, section * count + target))
    return lax.ppermute(value, ("section", "tp"), pairs)


def after(value, *earlier):
    return lax.optimization_barrier((value, *earlier))[0]


def from_next_section(value):
    count = lax.axis_size("section")
    return lax.ppermute(value, "section", [(i, (i - 1) % count) for i in range(count)])


def spread(pieces, steps, *earlier):
    for i in steps:
        parent, *links = TREE[i - 1]
        value = after(pieces[parent], *earlier) if earlier else pieces[parent]
        pieces[i] = along(value, links)


def returned(value, piece, until=0):
    paths = ["", ""]
    while piece != until:
        piece, *links = TREE[piece - 1]
        paths = [path + BACK[link] for path, link in zip(paths, links, strict=True)]
    return along(value, paths)


def lanes(block):
    return pl.ds(pl.multiple_of(block * SIDE, SIDE), SIDE)


def rounded_up(value, step):
    return -(-value // step) * step


def group_lists(index, count, key_column, width):
    length = index.shape[0]
    key, other = index[:, key_column], index[:, 1 - key_column]
    entry = jnp.arange(length, dtype=jnp.int32)
    live = entry < count
    same = (key[:, None] == key[None, :]) & live[None, :] & (entry[None, :] < entry[:, None])
    rank = jnp.sum(same.astype(jnp.int32), axis=1)
    opens = live & (rank % PAIR == 0)
    before = jnp.sum(((key[None, :] < key[:, None]) & opens[None, :]).astype(jnp.int32), axis=1)
    place = jnp.where(live, before * PAIR + rank, -1)
    at = jnp.arange(width, dtype=jnp.int32)
    empty = length * 32
    code = entry * 32 + other - empty
    codes = empty + jnp.sum(jnp.where(place[:, None] == at[None, :], code[:, None], 0), axis=0)
    keys = jnp.sum(jnp.where(place[:, None] == at[None, :] * PAIR, key[:, None], 0), axis=0)
    return codes, keys


def normed_kernel(inputs_ref, gain_ref, units_ref):
    for start in range(0, units_ref.shape[0], 16):
        at = pl.ds(start, 16)
        value = inputs_ref[at, :].astype(F32)
        rms_inv = lax.rsqrt(jnp.mean(value * value, axis=-1, keepdims=True) + EPS)
        units_ref[at, :] = (value * rms_inv * gain_ref[...]).astype(BF16)


def row_blocks(rows, features):
    return pl.BlockSpec((rows, features), lambda i: (i, 0))


def normed_units(inputs, gain):
    rows, features = inputs.shape
    return pl.pallas_call(
        normed_kernel,
        out_shape=jax.ShapeDtypeStruct((rows, features), BF16),
        grid=(rows // 32,),
        in_specs=[row_blocks(32, features), pl.BlockSpec((1, features), lambda i: (0, 0))],
        out_specs=row_blocks(32, features),
        compiler_params=pltpu.CompilerParams(vmem_limit_bytes=ROOM),
        cost_estimate=SMALL,
    )(inputs, gain)


def run_groups(count, unroll, one):
    whole = count // unroll

    @pl.loop(0, whole)
    def _(i):
        for j in range(unroll):
            one(i * unroll + j)

    for s in range(whole * unroll, count):
        one(s)


def start_tiles(tiles_ref, held, sem):
    count = tiles_ref.shape[0]
    copy = pltpu.make_async_copy(tiles_ref, held.at[pl.ds(0, count)], sem)
    copy.start()
    held[count] = jnp.zeros(held.shape[1:], BF16)
    return copy


def hidden_kernel(groups, codes_ref, keys_ref, *refs):
    unit_refs, (up_ref, hidden_ref, slope_ref, units, up, pre, sems) = refs[:PIECES], refs[PIECES:]
    rows = units.shape[0] // PIECES
    copies = [start_tiles(up_ref, up, sems.at[PIECES])]
    for i, ref in enumerate(unit_refs):
        copies.append(
            pltpu.make_async_copy(
                ref, units.at[pl.ds(i * rows, rows)], sems.at[i]
            )
        )
        copies[-1].start()
    pre[...] = jnp.zeros_like(pre)
    for copy in copies:
        copy.wait()

    def add(s):
        codes = [codes_ref[0, s * PAIR + i] for i in range(PAIR)]
        left = jnp.concatenate([units[:, lanes(code & 31)] for code in codes], axis=1)
        right = jnp.concatenate([up[code >> 5] for code in codes], axis=0)
        pre[:, lanes(keys_ref[0, s])] += jnp.dot(left, right, preferred_element_type=F32)

    run_groups(groups, 28, add)

    @pl.loop(0, pre.shape[0] // 32)
    def _(i):
        at = pl.ds(pl.multiple_of(i * 32, 32), 32)
        z = pre[at, :]
        square = z * z
        inner = jnp.tanh(GELU_C * (z + 0.044715 * square * z))
        hidden_ref[at, :] = (0.5 * z * (1.0 + inner)).astype(BF16)
        slope_ref[at, :] = 0.5 * (1.0 + inner) + 0.5 * z * (1.0 - inner * inner) * GELU_C * (
            1.0 + 3.0 * 0.044715 * square
        )


def hidden_of(codes, keys, units, up_tiles, unit_blocks, groups):
    rows, features = units[0].shape
    tokens, wide = PIECES * rows, unit_blocks * SIDE
    held = (up_tiles.shape[0] + 1,) + up_tiles.shape[1:]
    return pl.pallas_call(
        functools.partial(hidden_kernel, groups),
        out_shape=[
            jax.ShapeDtypeStruct((tokens, wide), BF16),
            jax.ShapeDtypeStruct((tokens, wide), F32),
        ],
        in_specs=[SMEM, SMEM] + [ANY] * (PIECES + 1),
        out_specs=[VMEM, VMEM],
        scratch_shapes=[
            pltpu.VMEM((tokens, features), BF16),
            pltpu.VMEM(held, BF16),
            pltpu.VMEM((tokens, wide), F32),
            pltpu.SemaphoreType.DMA((PIECES + 1,)),
        ],
        compiler_params=pltpu.CompilerParams(vmem_limit_bytes=ROOM),
        cost_estimate=SMALL,
    )(codes, keys, *units, up_tiles)


def pre_grad_kernel(pieces, start, groups, codes_ref, keys_ref, *refs):
    grad_refs, (down_ref, slope_ref, pre_grad_ref) = refs[:pieces], refs[pieces : pieces + 3]
    grads, down, slope, hidden_grad, sems = refs[pieces + 3 :]
    rows = grad_refs[0].shape[0]
    copies = [start_tiles(down_ref, down, sems.at[pieces])]
    for i, ref in enumerate(grad_refs):
        copies.append(
            pltpu.make_async_copy(ref, grads.at[pl.ds(i * rows, rows)], sems.at[i])
        )
        copies[-1].start()
    late = pltpu.make_async_copy(
        slope_ref.at[pl.ds(start, slope.shape[0])], slope, sems.at[pieces + 1]
    )
    late.start()
    hidden_grad[...] = jnp.zeros_like(hidden_grad)
    for copy in copies:
        copy.wait()

    def add(s):
        codes = [codes_ref[1, s * PAIR + i] for i in range(PAIR)]
        left = jnp.concatenate([grads[:, lanes(code & 31)] for code in codes], axis=1)
        right = jnp.concatenate([down[code >> 5] for code in codes], axis=1)
        hidden_grad[:, lanes(keys_ref[1, s])] += lax.dot_general(
            left, right, (((1,), (1,)), ((), ())), preferred_element_type=F32
        )

    run_groups(groups, 28, add)
    late.wait()

    @pl.loop(0, slope.shape[0] // 32)
    def _(i):
        at = pl.ds(pl.multiple_of(i * 32, 32), 32)
        pre_grad_ref[at, :] = (hidden_grad[at, :] * slope[at, :]).astype(BF16)


def pre_grad_of(codes, keys, grads, down_tiles, slope, groups, start=0):
    pieces = len(grads)
    rows, features = grads[0].shape
    tokens, wide = pieces * rows, slope.shape[1]
    held = (down_tiles.shape[0] + 1,) + down_tiles.shape[1:]
    return pl.pallas_call(
        functools.partial(pre_grad_kernel, pieces, start, groups),
        out_shape=jax.ShapeDtypeStruct((tokens, wide), BF16),
        in_specs=[SMEM, SMEM] + [ANY] * (pieces + 2),
        out_specs=VMEM,
        scratch_shapes=[
            pltpu.VMEM((tokens, features), BF16),
            pltpu.VMEM(held, BF16),
            pltpu.VMEM((tokens, wide), F32),
            pltpu.VMEM((tokens, wide), F32),
            pltpu.SemaphoreType.DMA((pieces + 2,)),
        ],
        compiler_params=pltpu.CompilerParams(vmem_limit_bytes=ROOM),
        cost_estimate=SMALL,
    )(codes, keys, *grads, down_tiles, slope)


def unit_grad_kernel(pieces, groups, codes_ref, keys_ref, pre_grad_ref, up_ref, *refs):
    out_refs, (up, total, sem) = refs[:pieces], refs[pieces:]
    rows = out_refs[0].shape[0]
    copy = start_tiles(up_ref, up, sem.at[0])
    total[...] = jnp.zeros_like(total)
    copy.wait()

    def add(s):
        codes = [codes_ref[2, s * PAIR + i] for i in range(PAIR)]
        left = jnp.concatenate([pre_grad_ref[:, lanes(code & 31)] for code in codes], axis=1)
        right = jnp.concatenate([up[code >> 5] for code in codes], axis=1)
        total[:, lanes(keys_ref[2, s])] += lax.dot_general(
            left, right, (((1,), (1,)), ((), ())), preferred_element_type=F32
        )

    run_groups(groups, 21, add)
    for piece, out_ref in enumerate(out_refs):

        @pl.loop(0, rows // 16)
        def _(i):
            step = pl.multiple_of(i * 16, 16)
            out_ref[pl.ds(step, 16), :] = total[pl.ds(piece * rows + step, 16), :].astype(BF16)


def unit_grad_of(codes, keys, pre_grad, up_tiles, rows, features, groups):
    tokens = pre_grad.shape[0]
    pieces = tokens // rows
    held = (up_tiles.shape[0] + 1,) + up_tiles.shape[1:]
    return pl.pallas_call(
        functools.partial(unit_grad_kernel, pieces, groups),
        out_shape=[jax.ShapeDtypeStruct((rows, features), BF16)] * pieces,
        in_specs=[SMEM, SMEM, VMEM, ANY],
        out_specs=[VMEM] * pieces,
        scratch_shapes=[
            pltpu.VMEM(held, BF16),
            pltpu.VMEM((tokens, features), F32),
            pltpu.SemaphoreType.DMA((1,)),
        ],
        compiler_params=pltpu.CompilerParams(vmem_limit_bytes=ROOM),
        cost_estimate=SMALL,
    )(codes, keys, pre_grad, up_tiles)


def both_grads_kernel(pieces, by_unit, by_feature, codes_ref, keys_ref, *refs):
    grad_refs, (down_ref, slope_ref, up_ref, pre_grad_ref) = refs[:pieces], refs[pieces : pieces + 4]
    out_refs = refs[pieces + 4 : 2 * pieces + 4]
    grads, down, slope, hidden_grad, up, total, sems = refs[2 * pieces + 4 :]
    rows = grad_refs[0].shape[0]
    copies = [start_tiles(down_ref, down, sems.at[pieces])]
    for i, ref in enumerate(grad_refs):
        copies.append(
            pltpu.make_async_copy(ref, grads.at[pl.ds(i * rows, rows)], sems.at[i])
        )
        copies[-1].start()
    slope_copy = pltpu.make_async_copy(slope_ref, slope, sems.at[pieces + 1])
    slope_copy.start()
    up_copy = start_tiles(up_ref, up, sems.at[pieces + 2])
    hidden_grad[...] = jnp.zeros_like(hidden_grad)
    total[...] = jnp.zeros_like(total)
    for copy in copies:
        copy.wait()

    def add_hidden_grad(s):
        codes = [codes_ref[1, s * PAIR + i] for i in range(PAIR)]
        left = jnp.concatenate([grads[:, lanes(code & 31)] for code in codes], axis=1)
        right = jnp.concatenate([down[code >> 5] for code in codes], axis=1)
        hidden_grad[:, lanes(keys_ref[1, s])] += lax.dot_general(
            left, right, (((1,), (1,)), ((), ())), preferred_element_type=F32
        )

    run_groups(by_unit, 28, add_hidden_grad)
    slope_copy.wait()

    @pl.loop(0, slope.shape[0] // 32)
    def _(i):
        at = pl.ds(pl.multiple_of(i * 32, 32), 32)
        pre_grad_ref[at, :] = (hidden_grad[at, :] * slope[at, :]).astype(BF16)

    up_copy.wait()

    def add_unit_grad(s):
        codes = [codes_ref[2, s * PAIR + i] for i in range(PAIR)]
        left = jnp.concatenate([pre_grad_ref[:, lanes(code & 31)] for code in codes], axis=1)
        right = jnp.concatenate([up[code >> 5] for code in codes], axis=1)
        total[:, lanes(keys_ref[2, s])] += lax.dot_general(
            left, right, (((1,), (1,)), ((), ())), preferred_element_type=F32
        )

    run_groups(by_feature, 21, add_unit_grad)
    for piece, out_ref in enumerate(out_refs):

        @pl.loop(0, rows // 16)
        def _(i):
            step = pl.multiple_of(i * 16, 16)
            out_ref[pl.ds(step, 16), :] = total[pl.ds(piece * rows + step, 16), :].astype(BF16)


def both_grads_of(codes, keys, grads, down_tiles, slope, up_tiles, by_unit, by_feature):
    pieces = len(grads)
    rows, features = grads[0].shape
    tokens, wide = slope.shape
    held = (up_tiles.shape[0] + 1,) + up_tiles.shape[1:]
    pre_grad, *parts = pl.pallas_call(
        functools.partial(both_grads_kernel, pieces, by_unit, by_feature),
        out_shape=[jax.ShapeDtypeStruct((tokens, wide), BF16)]
        + [jax.ShapeDtypeStruct((rows, features), BF16)] * pieces,
        in_specs=[SMEM, SMEM] + [ANY] * (pieces + 3),
        out_specs=[VMEM] * (1 + pieces),
        scratch_shapes=[
            pltpu.VMEM((tokens, features), BF16),
            pltpu.VMEM(held, BF16),
            pltpu.VMEM((tokens, wide), F32),
            pltpu.VMEM((tokens, wide), F32),
            pltpu.VMEM(held, BF16),
            pltpu.VMEM((tokens, features), F32),
            pltpu.SemaphoreType.DMA((pieces + 3,)),
        ],
        compiler_params=pltpu.CompilerParams(vmem_limit_bytes=ROOM),
        cost_estimate=SMALL,
    )(codes, keys, *grads, down_tiles, slope, up_tiles)
    return pre_grad, parts


def up_grad_kernel(parts, groups, codes_ref, keys_ref, *refs):
    pieces = 2 * PIECES
    unit_refs, slope_refs = refs[:pieces], refs[pieces : pieces + parts]
    out_ref, units, slopes, held, sems = refs[pieces + parts :]
    rows, done = unit_refs[0].shape[0], 0
    copies = []
    for i, ref in enumerate(slope_refs):
        size = ref.shape[0]
        copies.append(
            pltpu.make_async_copy(ref, slopes.at[pl.ds(done, size)], sems.at[pieces + i])
        )
        done += size
    for i, ref in enumerate(unit_refs):
        copies.append(
            pltpu.make_async_copy(ref, units.at[pl.ds(i * rows, rows)], sems.at[i])
        )
    for copy in copies:
        copy.start()
    held[...] = jnp.zeros_like(held)
    for copy in copies:
        copy.wait()

    def one(s):
        codes = [codes_ref[0, s * PAIR + i] for i in range(PAIR)]
        left = jnp.concatenate([units[:, lanes(code & 31)] for code in codes], axis=1)
        summed = lax.dot_general(
            left,
            slopes[:, lanes(keys_ref[0, s])],
            (((0,), (0,)), ((), ())),
            preferred_element_type=F32,
        ).astype(BF16)
        for i, code in enumerate(codes):
            held[code >> 5] = summed[i * SIDE : (i + 1) * SIDE]

    run_groups(groups, 14, one)
    copy = pltpu.make_async_copy(held.at[pl.ds(0, out_ref.shape[0])], out_ref, sems.at[0])
    copy.start()
    copy.wait()


def up_grad_of(codes, keys, units, slopes, count, groups):
    pieces = len(units)
    rows, features = units[0].shape
    tokens, wide = pieces * rows, slopes[0].shape[1]
    return pl.pallas_call(
        functools.partial(up_grad_kernel, len(slopes), groups),
        out_shape=jax.ShapeDtypeStruct((count, SIDE, SIDE), BF16),
        in_specs=[SMEM, SMEM] + [ANY] * (pieces + len(slopes)),
        out_specs=ANY,
        scratch_shapes=[
            pltpu.VMEM((tokens, features), BF16),
            pltpu.VMEM((tokens, wide), BF16),
            pltpu.VMEM((count + 1, SIDE, SIDE), BF16),
            pltpu.SemaphoreType.DMA((pieces + len(slopes),)),
        ],
        compiler_params=pltpu.CompilerParams(vmem_limit_bytes=ROOM),
        cost_estimate=SMALL,
    )(codes, keys, *units, *slopes)


def down_grad_kernel(groups, codes_ref, keys_ref, *refs):
    pieces = 2 * PIECES
    grad_refs, hidden_refs = refs[:pieces], refs[pieces : pieces + 2]
    out_ref, grads, hidden, turned, held, sems = refs[pieces + 2 :]
    rows, half = grad_refs[0].shape[0], hidden_refs[0].shape[0]
    copies = []
    for i, ref in enumerate(hidden_refs):
        copies.append(pltpu.make_async_copy(ref, hidden.at[pl.ds(i * half, half)], sems.at[i]))
    late = []
    for i, ref in enumerate(grad_refs):
        late.append(
            pltpu.make_async_copy(ref, grads.at[pl.ds(i * rows, rows)], sems.at[2 + i])
        )
    for copy in copies + late:
        copy.start()
    held[...] = jnp.zeros_like(held)
    for copy in copies:
        copy.wait()

    @pl.loop(0, turned.shape[0])
    def _(c):
        turned[c] = hidden[:, lanes(c)].T

    for copy in late:
        copy.wait()

    def one(s):
        codes = [codes_ref[1, s * PAIR + i] for i in range(PAIR)]
        right = jnp.concatenate([grads[:, lanes(code & 31)] for code in codes], axis=1)
        summed = jnp.dot(turned[keys_ref[1, s]], right, preferred_element_type=F32).astype(BF16)
        for i, code in enumerate(codes):
            held[code >> 5] = summed[:, i * SIDE : (i + 1) * SIDE]

    run_groups(groups, 14, one)
    copy = pltpu.make_async_copy(held.at[pl.ds(0, out_ref.shape[0])], out_ref, sems.at[0])
    copy.start()
    copy.wait()


def down_grad_of(codes, keys, grads, hidden, count, groups):
    pieces = len(grads)
    rows, features = grads[0].shape
    tokens, wide = pieces * rows, hidden[0].shape[1]
    return pl.pallas_call(
        functools.partial(down_grad_kernel, groups),
        out_shape=jax.ShapeDtypeStruct((count, SIDE, SIDE), BF16),
        in_specs=[SMEM, SMEM] + [ANY] * (pieces + 2),
        out_specs=ANY,
        scratch_shapes=[
            pltpu.VMEM((tokens, features), BF16),
            pltpu.VMEM((tokens, wide), BF16),
            pltpu.VMEM((wide // SIDE, SIDE, tokens), BF16),
            pltpu.VMEM((count + 1, SIDE, SIDE), BF16),
            pltpu.SemaphoreType.DMA((2 + pieces,)),
        ],
        compiler_params=pltpu.CompilerParams(vmem_limit_bytes=ROOM),
        cost_estimate=SMALL,
    )(codes, keys, *grads, *hidden)


def input_grad_kernel(inputs_ref, gain_ref, grad_ref, *refs):
    term_refs, out_ref = refs[:-1], refs[-1]
    for start in range(0, out_ref.shape[0], 16):
        here = pl.ds(start, 16)
        value = inputs_ref[here, :].astype(F32)
        rms_inv = lax.rsqrt(jnp.mean(value * value, axis=-1, keepdims=True) + EPS)
        normed = value * rms_inv
        unit_grad = term_refs[0][here, :].astype(F32)
        for ref in term_refs[1:]:
            unit_grad = unit_grad + ref[here, :].astype(F32)
        scaled = unit_grad * gain_ref[...]
        mean = jnp.mean(scaled * normed, axis=-1, keepdims=True)
        result = grad_ref[here, :].astype(F32) + rms_inv * (scaled - normed * mean)
        out_ref[here, :] = result.astype(BF16)


def input_grad_of(inputs, gain, arriving, terms):
    rows, features = inputs.shape
    return pl.pallas_call(
        input_grad_kernel,
        out_shape=jax.ShapeDtypeStruct((rows, features), BF16),
        grid=(rows // 32,),
        in_specs=[row_blocks(32, features), pl.BlockSpec((1, features), lambda i: (0, 0))]
        + [row_blocks(32, features)] * (1 + len(terms)),
        out_specs=row_blocks(32, features),
        compiler_params=pltpu.CompilerParams(vmem_limit_bytes=ROOM),
        cost_estimate=SMALL,
    )(inputs, gain, arriving, *terms)


def body(
    inputs,
    norm_gain,
    incoming_grad,
    up_tiles,
    up_index,
    up_count,
    down_tiles,
    down_index,
    down_count,
):
    up, down = up_tiles[0], down_tiles[0]
    rows, features = inputs.shape[1:]
    count = up.shape[0]
    feature_blocks = features // SIDE
    unit_blocks = FF // lax.axis_size("tp") // SIDE
    by_unit = (count + unit_blocks * (PAIR - 1)) // PAIR
    by_feature = (count + feature_blocks * (PAIR - 1)) // PAIR
    width = rounded_up(PAIR * by_feature, SIDE)

    near, far = range(PIECES), range(PIECES, 2 * PIECES)

    units = {0: normed_units(inputs[0], norm_gain)}
    spread(units, (1, 2, 3))
    arriving = from_next_section(incoming_grad[0])
    lists = [
        group_lists(up_index[0], up_count[0, 0], 1, width),
        group_lists(down_index[0], down_count[0, 0], 0, width),
        group_lists(up_index[0], up_count[0, 0], 0, width),
    ]
    codes = jnp.stack([pair[0] for pair in lists])
    keys = jnp.stack([pair[1] for pair in lists])

    spread(units, (5, 4, 6), units[1], units[2], units[3])
    near_hidden, near_slope = hidden_of(
        codes, keys, [units[i] for i in near], up, unit_blocks, by_unit
    )
    last = (near_slope, units[4], units[5], units[6])
    spread(units, (7,), *last)
    grads = {0: after(arriving, *last)}
    spread(grads, (1, 2, 3))
    far_hidden, far_slope = hidden_of(
        codes, keys, [units[i] for i in far], up, unit_blocks, by_unit
    )
    spread(grads, (5, 4, 6), far_slope, grads[1], grads[2], grads[3])
    near_pre_grad = pre_grad_of(
        after(codes, far_slope), keys, [grads[i] for i in near], down, near_slope, by_unit
    )
    spread(grads, (7,), near_pre_grad)
    parts = unit_grad_of(
        after(codes, grads[4], grads[5]), keys, near_pre_grad, up, rows, features, by_feature
    )
    terms = [parts[0]] + [returned(after(parts[i], grads[6]), i) for i in (1, 2, 3)]
    far_pre_grad, far_parts = both_grads_of(
        after(codes, *parts, grads[7]),
        keys,
        [grads[i] for i in far],
        down,
        far_slope,
        up,
        by_unit,
        by_feature,
    )
    parts = [*parts, *far_parts]
    terms += [returned(after(parts[i], *terms[1:4]), i) for i in (7, 4, 5, 6)]
    pre_grads, hidden = [near_pre_grad, far_pre_grad], [near_hidden, far_hidden]
    up_grad = up_grad_of(
        after(codes, *parts), keys, [units[i] for i in range(2 * PIECES)], pre_grads, count, by_unit
    )
    down_grad = down_grad_of(
        after(codes, up_grad), keys, [grads[i] for i in range(2 * PIECES)], hidden, count, by_unit
    )
    input_grad = input_grad_of(inputs[0], norm_gain, arriving, terms)
    return (input_grad[None], up_grad[None], down_grad[None])


def solution(mesh):
    placed = (
        P("section", "tp", None),
        P("section", None),
        P("section", "tp", None),
        P("section", "tp", None, None),
        P("section", "tp", None),
        P("section", "tp"),
        P("section", "tp", None, None),
        P("section", "tp", None),
        P("section", "tp"),
    )
    return jax.shard_map(
        body,
        mesh=mesh,
        in_specs=placed,
        out_specs=(
            P("section", "tp", None),
            P("section", "tp", None, None),
            P("section", "tp", None, None),
        ),
        check_vma=False,
    )
```
